512 devices in a mesh: ctx: 64 (over x, z), tp: 8 (over y, core).
Axes of the slice: x: 4, y: 4, z: 16, core: 2. Of those that a mesh axis runs over, the one named last changes fastest.
Arguments:
- queries: bfloat16 [12288, 8192], P('ctx', 'tp'), may hold values from -16 to 16
- keys: bfloat16 [12288, 1024], P('ctx', 'tp'), may hold values from -4 to 4
- values: bfloat16 [12288, 1024], P('ctx', 'tp'), may hold values from -5 to 5
- lengths: int32 [64], replicated, may hold values from 1 to 192, 9216 in all
- page_owner: int32 [6144, 1], P('ctx'), may hold values from 0 to 63; in each aligned block of 96 rows (0 to 95, 96 to 191, ...) at most 2 rows name the same one
Outputs:
- attended: bfloat16 [12288, 8192], P('ctx', 'tp')
- decode_cache: bfloat16 [64, 128, 2, 8, 256], P('ctx', 'tp')
The draws below stay inside these ranges and needn't reach their ends.
Inputs may be any that keep to these rules, and one draw needn't show every extreme that they name: The lengths sum to 9216; the largest is exactly 192. `page_owner`: among the pages of one index of ctx no owner is named more than 2 times.
All inputs are finite; a program needn't handle non-finite values.
Results may differ from the reference program's by a relative error of at most 0.0065.
Values may be sent and summed in bfloat16 or wider, within the bound.
No kernel may reach another device: no remote copies, remote signals or barrier semaphores. Data moves between devices by JAX's collectives and lax.ppermute only.
A program may use at most 64 MiB of HBM per device.

```python
import math
import jax
import jax.numpy as jnp
import numpy as np
from jax import lax

HQ = 64
KVH = 8
HD = 128
CAP = 192
PAGE = 2
PAGES_DEV = 96
SLOTS = 2
TOKENS = 12288
TOTAL_LEN = 9216
N_CTX = 64


def draw_keys(key, part):
    key = jax.random.fold_in(key, 11)
    base = jnp.clip(jax.random.normal(key, (TOKENS, KVH * HD), jnp.float32), -4.0, 4.0)
    return base.astype(jnp.bfloat16)


def draw_queries(key, part):
    key = jax.random.fold_in(key, 23)
    base = jnp.clip(jax.random.normal(key, (TOKENS, HQ * HD), jnp.float32), -4.0, 4.0)
    return base.astype(jnp.bfloat16)


def block_scale(own_key, shape, cuts, least, largest):
    def one(position, parts):
        heights = jax.random.uniform(jax.random.fold_in(jax.random.fold_in(own_key, 6), position), (parts,), jnp.float32, least / len(cuts), largest / len(cuts))
        return jnp.repeat(jnp.exp(heights), shape[position] // parts).reshape((-1,) + (1,) * (len(shape) - position - 1))

    level = one(*cuts[0])
    for cut in cuts[1:]:
        level = level * one(*cut)
    return level


def profile(amount, total, limit, slope):
    loads = [(1 << 20) // math.isqrt(grade ** slope) + 1 for grade in range(2, amount + 1)]
    surplus, counts = total - limit - (amount - 1), [1] * (amount - 1)
    while surplus > 0:
        free = [i for i in range(amount - 1) if counts[i] < limit]
        mass, remaining = sum([loads[i] for i in free]), surplus
        for i in free:
            addition = min(limit - counts[i], max(1, remaining * loads[i] // mass), surplus)
            counts[i] = counts[i] + addition
            surplus = surplus - addition
    return np.array([limit] + counts)


def ragged_sizes(key, number_of, total, most, skew):
    if number_of == 2:
        one = jax.random.randint(key, (), max(1, total - most), min(most, total - 1) + 1)
        return jnp.stack([one, total - one])
    sizes = jnp.asarray(profile(number_of, total, most, skew), jnp.int32)
    twos = (number_of - 1) // 2
    giver, receiver = sizes[1:1 + 2 * twos:2], sizes[2:2 + 2 * twos:2]
    room = jnp.minimum(giver - 1, most - receiver)
    passed = jax.random.randint(jax.random.fold_in(key, 1), (twos,), 0, 1 << 20) % (room + 1)
    sizes = sizes.at[1:1 + 2 * twos:2].set(giver - passed).at[2:2 + 2 * twos:2].set(receiver + passed)
    return sizes[jax.random.permutation(jax.random.fold_in(key, 2), number_of)]


def assign_block(own_key, own, number, rows, amount, top, limit, slope):
    sequence = jax.random.permutation(own_key, amount)
    packed, common = load_shares(amount, rows * top, limit, slope, True), load_shares(amount, rows * top, limit, slope, False)
    places = jnp.arange(amount)

    def named(sizes, offset_by):
        used = int((sizes > 0).sum())
        fixed = max(1, used // 4)
        moved = fixed + (places - fixed + offset_by * (used - fixed)) % max(1, amount - fixed)
        return jnp.zeros((amount,), jnp.int32).at[sequence[jnp.where(places < fixed, places, moved)]].set(jnp.asarray(sizes, jnp.int32))

    sizes = jnp.where(number % 4 == 0, named(packed, number // 4), named(common, number - number // 4 - 1))
    mixed = jax.random.permutation(jax.random.fold_in(own, 3), amount)
    source_of, taker = mixed[0:amount // 2 * 2:2], mixed[1:amount // 2 * 2:2]
    margin = jnp.minimum(sizes[source_of] - 1, limit - sizes[taker]) // 2
    margin = jnp.where((source_of == sequence[0]) | (taker == sequence[0]) | (sizes[taker] == 0), 0, jnp.maximum(margin, 0))
    moved = jax.random.randint(jax.random.fold_in(own, 4), (amount // 2,), 0, 1 << 20) % (margin + 1)
    sizes = sizes.at[source_of].add(-moved).at[taker].add(moved)
    members = jnp.searchsorted(jnp.cumsum(sizes), jnp.arange(rows * top), side="right").astype(jnp.int32)
    grid = members.reshape(top, rows).T
    grid = grid[jax.random.permutation(jax.random.fold_in(own, 1), rows)]
    offset_by = jax.random.randint(jax.random.fold_in(own, 2), (rows, 1), 0, top)
    return jnp.take_along_axis(grid, (jnp.arange(top)[None, :] + offset_by) % top, axis=1)


def load_shares(amount, total, limit, lean, full):
    loads = [(1 << 20) // math.isqrt(rank ** lean) + 1 for rank in range(1, amount + 1)]
    largest = limit if full else min(limit, max(-(-total // amount), total * loads[0] // sum(loads)))
    least = 1 if total - largest >= amount - 1 else 0
    counts, rest = [largest] + [least] * (amount - 1), total - largest - least * (amount - 1)
    while rest > 0:
        free = [i for i in range(1, amount) if counts[i] < largest] or [i for i in range(1, amount) if counts[i] < limit]
        mass, remaining = sum([loads[i] for i in free]), rest
        for i in free:
            addition = min(limit - counts[i], max(1, remaining * loads[i] // mass), rest)
            counts[i] = counts[i] + addition
            rest = rest - addition
    return np.array(counts)


def bell_draw(rng, shape, scale, bound, split=(), kind=jnp.bfloat16):
    values = jax.random.normal(rng, shape, jnp.float32) * scale
    if len(split) > 0:
        values = block_scale(rng, shape, split, -0.22, 0.18) * values
    return jnp.clip(values, min=-bound, max=bound).astype(kind)


def setup_inputs(seed: int = 0) -> dict:
    splits = jax.random.split(jax.random.key(seed), 6)
    queries = draw_queries(jax.random.fold_in(splits[5], 71), 0)
    keys = draw_keys(jax.random.fold_in(splits[5], 71), 0)
    values = bell_draw(splits[2], (TOKENS, KVH * HD), 1.0, 5.0, ((0, 64), (1, 8)))
    lengths = ragged_sizes(splits[3], N_CTX, TOTAL_LEN, CAP, 2).astype(jnp.int32)
    page_owner_keys = jax.random.split(jax.random.fold_in(splits[4], 1), (TOKENS // PAGE) // PAGES_DEV)
    page_owner_turns = jax.random.permutation(jax.random.fold_in(splits[4], 3), (TOKENS // PAGE) // PAGES_DEV)
    page_owner = jax.vmap(lambda own, number: assign_block(jax.random.fold_in(splits[4], 2), own, number, PAGES_DEV, N_CTX, 1, SLOTS, 2))(page_owner_keys, page_owner_turns).reshape((TOKENS // PAGE, 1))
    return dict(queries=queries, keys=keys, values=values, lengths=lengths, page_owner=page_owner)


def span_attention(q_span, key_rows, value_rows, q_pos, q_ok, k_pos, k_ok):
    scale = 1.0 / math.sqrt(HD)
    group = HQ // KVH
    q_view = q_span.reshape(q_span.shape[0], KVH, group, HD).transpose(1, 0, 2, 3)
    k_view = key_rows.reshape(key_rows.shape[0], KVH, HD).transpose(1, 0, 2)
    v_view = value_rows.reshape(value_rows.shape[0], KVH, HD).transpose(1, 0, 2)
    allowed = ((k_pos[None, :] <= q_pos[:, None]) & k_ok[None, :])[:, None, :]

    def one_head(items):
        q_head, k_head, v_head = items
        scores = jnp.einsum('rgd,kd->rgk', q_head.astype(jnp.float32), k_head.astype(jnp.float32)) * scale
        top = lax.optimization_barrier(jnp.max(jnp.where(allowed, scores, -1e+30), axis=-1, keepdims=True))
        weights = jnp.where(allowed, jnp.exp(scores - top), 0.0)
        total = lax.optimization_barrier(jnp.sum(weights, axis=-1))
        rounded = weights.astype(jnp.bfloat16).astype(jnp.float32)
        numer = jnp.einsum('rgk,kd->rgd', rounded, v_head.astype(jnp.float32))
        safe = jnp.where(q_ok[:, None], total, 1.0)
        return jnp.where(q_ok[:, None, None], numer / safe[:, :, None], 0.0)
    result = lax.map(one_head, (q_view, k_view, v_view))
    return result.transpose(1, 0, 2, 3).reshape(q_span.shape[0], HQ * HD).astype(jnp.bfloat16)

def reference(queries, keys, values, lengths, page_owner):
    offsets = jnp.cumsum(lengths) - lengths
    rows = jnp.arange(CAP, dtype=jnp.int32)
    pieces = []
    for index in range(N_CTX):
        count = (index + 1) * CAP
        q_pos = offsets[index] + rows
        q_ok = rows < lengths[index]
        key_index = jnp.arange(count, dtype=jnp.int32)
        source = key_index // CAP
        local = key_index - source * CAP
        k_pos = offsets[source] + local
        k_ok = local < lengths[source]
        pieces.append(span_attention(queries[index * CAP:(index + 1) * CAP], keys[:count], values[:count], q_pos, q_ok, k_pos, k_ok))
    attended = jnp.concatenate(pieces, axis=0)
    page_index = jnp.arange(PAGES_DEV, dtype=jnp.int32)
    paged = jnp.concatenate([keys.reshape(N_CTX, PAGES_DEV, PAGE, KVH, HD), values.reshape(N_CTX, PAGES_DEV, PAGE, KVH, HD)], axis=-1)
    finished = (page_index[None, :] + 1) * PAGE <= lengths[:, None]
    paged = jnp.where(finished[:, :, None, None, None], paged, jnp.zeros_like(paged))
    owner = page_owner.reshape(N_CTX, PAGES_DEV)
    same = owner[:, :, None] == owner[:, None, :]
    earlier = page_index[None, :] < page_index[:, None]
    rank = lax.optimization_barrier(jnp.sum((same & earlier[None]).astype(jnp.int32), axis=2))
    slot = jnp.arange(N_CTX, dtype=jnp.int32)[:, None] * SLOTS + rank
    decode_cache = jnp.zeros((N_CTX, N_CTX * SLOTS, PAGE, KVH, 2 * HD), jnp.bfloat16).at[owner, slot].set(paged)
    return (attended, decode_cache)
```

```python
import functools
import math

import jax
import jax.numpy as jnp
from jax import lax
from jax.experimental import pallas as pl
from jax.experimental.pallas import tpu as pltpu
from jax.sharding import PartitionSpec as P

HD = 128
PAGE = 2
NX = 4
NZ = 16
N = NX * NZ
CAP = 192
HALF = CAP // 2
PAGES = CAP // PAGE
HALF_PAGES = PAGES // 2
ROWS_A = 2 * HALF
ROWS_B = 2 * HALF + 16
GROUP = 8
BLOCK = 8
WIDTH = BLOCK * HALF
BLOCKS = 2 * N // BLOCK
NEG = -1e30

X_GROUPS = [[x * NZ + z for x in range(NX)] for z in range(NZ)]
Z_GROUPS = [[x * NZ + z for z in range(NZ)] for x in range(NX)]


def shift(value, dx, dz):
    pairs = [
        (x * NZ + z, ((x + dx) % NX) * NZ + (z + dz) % NZ) for x in range(NX) for z in range(NZ)
    ]
    return lax.ppermute(value, "ctx", pairs)


def attention_kernel(n_ref, q_ref, k_ref, v_ref, bias_ref, *refs):
    sources, (out_ref, qs, kv, m, l, acc, sems) = refs[:6], refs[6:]
    copies = []
    start = 0
    for i, source in enumerate(sources):
        count, rows = source.shape[0], source.shape[1]
        copies.append(
            pltpu.make_async_copy(
                source, kv.at[pl.ds(start, count), pl.ds(0, rows)], sems.at[i]
            )
        )
        start += count
    for copy in copies:
        copy.start()
    scale = math.log2(math.e) / math.sqrt(HD)
    live = n_ref[0]

    for h in range(GROUP):
        qs[h] = q_ref[:, h * HD : (h + 1) * HD]

    row = lax.broadcasted_iota(jnp.int32, (CAP, CAP), 0)
    col = lax.broadcasted_iota(jnp.int32, (CAP, CAP), 1)
    own_bias = jnp.where((col <= row) & (col < live), 0.0, NEG).astype(jnp.float32)
    keys = k_ref[...]
    values = v_ref[...]

    def scores(h, keys, bias):
        s = lax.dot_general(
            qs[h], keys, (((1,), (1,)), ((), ())), preferred_element_type=jnp.float32
        )
        return s * scale + bias

    def own(h, carry):
        s = scores(h, keys, own_bias)
        top = jnp.max(s, axis=1, keepdims=True)
        p = jnp.exp2(s - top)
        m[h] = jnp.broadcast_to(top, (CAP, HD))
        l[h] = jnp.broadcast_to(jnp.sum(p, axis=1, keepdims=True), (CAP, HD))
        acc[h] = jnp.dot(p.astype(jnp.bfloat16), values, preferred_element_type=jnp.float32)
        return carry

    lax.fori_loop(0, GROUP, own, 0)

    for copy in copies:
        copy.wait()

    def block(b, carry):
        def head(h, inner):
            first = pl.multiple_of(b * BLOCK, BLOCK)
            k = kv[pl.ds(first, BLOCK), 0:HALF, :].reshape(WIDTH, HD)
            v = kv[pl.ds(first, BLOCK), HALF : 2 * HALF, :].reshape(WIDTH, HD)
            s = scores(h, k, bias_ref[b])
            old = m[h][:, :1]
            top = jnp.maximum(old, jnp.max(s, axis=1, keepdims=True))
            p = jnp.exp2(s - top)
            factor = jnp.exp2(old - top)
            m[h] = jnp.broadcast_to(top, (CAP, HD))
            l[h] = l[h] * factor + jnp.sum(p, axis=1, keepdims=True)
            acc[h] = acc[h] * factor + jnp.dot(
                p.astype(jnp.bfloat16), v, preferred_element_type=jnp.float32
            )
            return inner

        return lax.fori_loop(0, GROUP, head, carry, unroll=2)

    lax.fori_loop(0, BLOCKS, block, 0)

    ok = lax.broadcasted_iota(jnp.int32, (CAP, HD), 0) < live
    for h in range(GROUP):
        result = jnp.where(ok, acc[h] / l[h], 0.0)
        out_ref[:, h * HD : (h + 1) * HD] = result.astype(jnp.bfloat16)


def attention(live, queries, keys, values, bias, sources):
    vmem = pl.BlockSpec(memory_space=pltpu.VMEM)
    return pl.pallas_call(
        attention_kernel,
        out_shape=jax.ShapeDtypeStruct(queries.shape, jnp.bfloat16),
        in_specs=[pl.BlockSpec(memory_space=pltpu.SMEM)]
        + [vmem] * 4
        + [pl.BlockSpec(memory_space=pl.ANY)] * len(sources),
        out_specs=vmem,
        scratch_shapes=[
            pltpu.VMEM((GROUP, CAP, HD), jnp.bfloat16),
            pltpu.VMEM((2 * N, ROWS_B, HD), jnp.bfloat16),
            pltpu.VMEM((GROUP, CAP, HD), jnp.float32),
            pltpu.VMEM((GROUP, CAP, HD), jnp.float32),
            pltpu.VMEM((GROUP, CAP, HD), jnp.float32),
            pltpu.SemaphoreType.DMA((len(sources),)),
        ],
        compiler_params=pltpu.CompilerParams(vmem_limit_bytes=40 * 1024 * 1024),
        cost_estimate=pl.CostEstimate(
            flops=4 * GROUP * CAP * N * CAP * HD, bytes_accessed=8 << 20, transcendentals=0
        ),
    )(live, queries, keys, values, bias, *sources)


def select_kernel(sel_ref, *refs):
    sources, (out_ref, pages, sems) = refs[:6], refs[6:]
    copies = []
    start = 0
    for i, source in enumerate(sources):
        count = source.shape[0]
        copies.append(
            pltpu.make_async_copy(source, pages.at[pl.ds(start, count)], sems.at[i])
        )
        start += count
    for copy in copies:
        copy.start()
    for copy in copies:
        copy.wait()

    def one(s, carry):
        place = sel_ref[s]
        found = jnp.maximum(place, 0)
        keep = jnp.where(place >= 0, 1.0, 0.0).astype(jnp.bfloat16)
        out_ref[s, :, 0:HD] = pages[found] * keep
        out_ref[s, :, HD : 2 * HD] = pages[found + HALF_PAGES] * keep
        return carry

    lax.fori_loop(0, 2 * N, one, 0, unroll=4)


def select_pages(sel, sources):
    total = sum(s.shape[0] for s in sources)
    return pl.pallas_call(
        select_kernel,
        out_shape=jax.ShapeDtypeStruct((2 * N, PAGE, 2 * HD), jnp.bfloat16),
        in_specs=[pl.BlockSpec(memory_space=pltpu.SMEM)]
        + [pl.BlockSpec(memory_space=pl.ANY)] * len(sources),
        out_specs=pl.BlockSpec(memory_space=pltpu.VMEM),
        scratch_shapes=[
            pltpu.VMEM((total, PAGE, HD), jnp.bfloat16),
            pltpu.SemaphoreType.DMA((len(sources),)),
        ],
        compiler_params=pltpu.CompilerParams(vmem_limit_bytes=40 * 1024 * 1024),
        cost_estimate=pl.CostEstimate(flops=0, bytes_accessed=8 << 20, transcendentals=0),
    )(sel, *sources)


def body(queries, keys, values, lengths, page_owner):
    me = lax.axis_index("ctx")
    mx, mz = me // NZ, me % NZ
    my_length = jnp.sum(jnp.where(jnp.arange(N, dtype=jnp.int32) == me, lengths, 0))

    page_index = jnp.arange(PAGES, dtype=jnp.int32)
    owner = page_owner[:, 0]
    same = owner[:, None] == owner[None, :]
    earlier = page_index[None, :] < page_index[:, None]
    rank = jnp.sum((same & earlier).astype(jnp.int32), axis=1)
    finished = (page_index + 1) * PAGE <= my_length
    slot = jnp.where(finished, owner * 2 + rank, -1)
    table = jnp.sum(
        jnp.where(
            slot[:, None] == jnp.arange(2 * N, dtype=jnp.int32)[None, :],
            page_index[:, None] + 1,
            0,
        ),
        axis=0,
    ).astype(jnp.bfloat16)

    a = jnp.concatenate([keys[:HALF], values[:HALF]], axis=0)
    b = jnp.concatenate(
        [keys[HALF:], values[HALF:], jnp.broadcast_to(table[None, :], (16, 2 * N))], axis=0
    )

    a = lax.all_gather(a, "ctx", axis=0, tiled=False, axis_index_groups=X_GROUPS)
    a = lax.all_gather(a, "ctx", axis=0, tiled=False, axis_index_groups=Z_GROUPS)
    a = a.reshape(N, ROWS_A, HD)

    up, down = [b], [b]
    for k in range(8):
        up.append(shift(up[-1], 0, 1))
        if k < 7:
            down.append(shift(down[-1], 0, -1))
    b0 = jnp.stack(up + down[1:])
    from_left = shift(b0, 1, 0)
    from_right = shift(b0, -1, 0)
    far_left = shift(from_left[:8], 1, 0)
    far_right = shift(from_right[8:], -1, 0)
    sources = [a, b0, from_left, from_right, far_left, far_right]

    order_z = [-k for k in range(9)] + list(range(1, 8))
    delta_z = jnp.array(order_z * NX, jnp.int32)
    delta_x = jnp.array([0] * NZ + [-1] * NZ + [1] * NZ + [2] * NZ, jnp.int32)
    piece_b = ((mx + delta_x) % NX) * NZ + (mz + delta_z) % NZ
    place = jnp.arange(N, dtype=jnp.int32)
    piece_a = (place % NX) * NZ + place // NX
    piece = jnp.concatenate([piece_a, piece_b])
    base = jnp.concatenate([jnp.zeros((N,), jnp.int32), jnp.full((N,), HALF, jnp.int32)])
    sizes = jnp.sum(jnp.where(piece[:, None] == place[None, :], lengths[None, :], 0), axis=1)
    count = jnp.where(piece < me, sizes - base, 0)
    bias = jnp.where(
        jnp.arange(HALF, dtype=jnp.int32)[None, :] < count[:, None], 0.0, NEG
    ).astype(jnp.float32)
    bias = bias.reshape(BLOCKS, 1, WIDTH)

    tables = jnp.concatenate([s[:, ROWS_A, :] for s in sources[1:]], axis=0)
    codes = lax.dynamic_slice(tables, (0, me * 2), (N, 2)).astype(jnp.int32)
    hit = piece_b[:, None] == place[None, :]
    code = jnp.sum(jnp.where(hit[:, :, None], codes[:, None, :], 0), axis=0)
    place_b = jnp.sum(jnp.where(hit, place[:, None], 0), axis=0)
    place_a = (place % NZ) * NX + place // NZ
    page = code - 1
    pages_a, pages_b = ROWS_A // PAGE, ROWS_B // PAGE
    at_a = place_a[:, None] * pages_a + page
    at_b = N * pages_a + place_b[:, None] * pages_b + page - HALF_PAGES
    sel = jnp.where(page < 0, -1, jnp.where(page < HALF_PAGES, at_a, at_b)).reshape(2 * N)

    outgoing = select_pages(
        sel, [s.reshape(s.shape[0] * s.shape[1] // PAGE, PAGE, HD) for s in sources]
    )
    decode_cache = lax.all_to_all(
        outgoing.reshape(2 * N, PAGE, 1, 2 * HD), "tp", split_axis=0, concat_axis=2, tiled=True
    )
    attended = attention(my_length.reshape(1), queries, keys, values, bias, sources)
    return (attended, decode_cache.reshape((1,) + decode_cache.shape))


def solution(mesh):
    in_specs = (P("ctx", "tp"), P("ctx", "tp"), P("ctx", "tp"), P(), P("ctx", None))
    out_specs = (P("ctx", "tp"), P("ctx", "tp", None, None, None))
    return jax.shard_map(body, mesh=mesh, in_specs=in_specs, out_specs=out_specs, check_vma=False)
```

```python
import math

import jax
import jax.numpy as jnp
from jax import lax
from jax.experimental import pallas as pl
from jax.experimental.pallas import tpu as pltpu
from jax.sharding import PartitionSpec as P

HD = 128
PAGE = 2
NX = 4
NZ = 16
N = NX * NZ
CAP = 192
ROWS_A = 64
ROWS_B = CAP - ROWS_A
PAGES = CAP // PAGE
PAGES_A = ROWS_A // PAGE
PAGES_B = ROWS_B // PAGE
PAD = 16
TALL_A = 2 * ROWS_A + PAD
TALL_B = 2 * ROWS_B
GROUP = 8
ROWS = GROUP * CAP
TILES = 4
TILE = ROWS // TILES
WIDTH = 512
DEAD = -1e30
SCALE = math.log2(math.e) / math.sqrt(HD)
LIMIT = 64.0 / SCALE
VMEM_LIMIT = 56 * 1024 * 1024

Z_GROUPS = [[x * NZ + z for z in range(NZ)] for x in range(NX)]
Z_FIRST = [4, 0, -4, 8]
Z_REST = [3, -1, -5, 7, 5, 1, -3, 9, -2, -6, 6, 2]
X_A = [0, -1, 1, 2]
X_B = [0] * 16 + [-1] * 4 + [1] * 4 + [-1] * 12 + [1] * 12 + [2] * 16
Z_B = (Z_FIRST + Z_REST) + Z_FIRST * 2 + Z_REST * 2 + (Z_FIRST + Z_REST)


def shift(value, dx, dz):
    pairs = [
        (x * NZ + z, ((x + dx) % NX) * NZ + (z + dz) % NZ) for x in range(NX) for z in range(NZ)
    ]
    return lax.ppermute(value, "ctx", pairs)


def gather_z(value):
    return lax.all_gather(value, "ctx", axis=0, tiled=False, axis_index_groups=Z_GROUPS)


def exchange(a, b):
    left4, right4 = shift(b, 0, 4), shift(b, 0, -4)
    near = [shift(a, dx, 0) for dx in (1, -1, 2)]
    far4 = jnp.concatenate(
        [shift(left4[:ROWS_B], 0, 4), shift(right4[ROWS_B:], 0, -4)], axis=0
    )
    first = jnp.stack([right4, b, left4, far4])
    gathered = gather_z(jnp.stack([a] + near)).reshape(N, TALL_A, HD)
    rest = jnp.concatenate(
        [shift(first, 0, 1), shift(first, 0, -1), shift(first[1:3], 0, 2), shift(first[0:2], 0, -2)],
        axis=0,
    )
    first_left, first_right = shift(first, 1, 0), shift(first, -1, 0)
    first_far = shift(first_left, 1, 0)
    rest_left, rest_right = shift(rest, 1, 0), shift(rest, -1, 0)
    far_left, far_right = shift(rest_left[:4], 1, 0), shift(rest_right[4:], -1, 0)
    own = [first, rest]
    beside = [first_left, first_right, rest_left, rest_right]
    across = [first_far, far_left, far_right]
    return gathered, own, beside, across


def lanes(rows):
    return lax.broadcasted_iota(jnp.int32, (rows, HD), 1)


def reference_columns(m):
    rows = m.shape[0]
    m = jnp.broadcast_to(m, (rows, HD))
    high = m.astype(jnp.bfloat16).astype(jnp.float32)
    rest = m - high
    middle = rest.astype(jnp.bfloat16).astype(jnp.float32)
    low = rest - middle
    lane = lanes(rows)
    out = jnp.where(lane == 0, 1.0, 0.0)
    out = jnp.where(lane == 1, -high, out)
    out = jnp.where(lane == 2, -middle, out)
    out = jnp.where(lane == 3, -low, out)
    return out.astype(jnp.bfloat16)


def dot_t(a, b):
    return lax.dot_general(a, b, (((1,), (1,)), ((), ())), preferred_element_type=jnp.float32)


def by_lanes(op, s):
    out = s[:, :HD]
    for i in range(1, s.shape[1] // HD):
        out = op(out, s[:, i * HD : (i + 1) * HD])
    return out


def attention_kernel(first, last, talls, counts, *refs):
    n_src = len(talls)
    count_ref, live_ref = refs[0], refs[1]
    sources = refs[2 : 2 + n_src]
    refs = refs[2 + n_src :]
    if first:
        (q_ref, k_ref, v_ref), refs = refs[:3], refs[3:]
    else:
        (q0, l0, acc0), refs = refs[:3], refs[3:]
    if last:
        out_ref, refs = refs[0], refs[1:]
    q1, l1, acc1, kbuf, vbuf, sems = refs[:6]
    stages, refs = refs[6 : 6 + n_src], refs[6 + n_src :]
    if first:
        q0, l0, acc0 = refs
    live = live_ref[0]

    copies = [
        pltpu.make_async_copy(sources[i], stages[i], sems.at[i]) for i in range(n_src)
    ]
    for copy in copies:
        copy.start()

    if first:
        row = lax.broadcasted_iota(jnp.int32, (CAP, CAP), 0)
        col = lax.broadcasted_iota(jnp.int32, (CAP, CAP), 1)
        bias = jnp.where((col <= row) & (col < live), 0.0, DEAD).astype(jnp.float32)
        for h in range(GROUP):
            at = slice(h * CAP, (h + 1) * CAP)
            q = q_ref[:, h * HD : (h + 1) * HD]
            s = dot_t(q, k_ref[...]) + bias
            top = jnp.max(s, axis=1, keepdims=True)
            p = jnp.exp2((s - top) * SCALE)
            q0[at, 0:HD] = q
            q0[at, HD : 2 * HD] = reference_columns(top)
            l0[at, :] = jnp.where(lanes(CAP) == 0, jnp.sum(p, axis=1, keepdims=True), 0.0)
            acc0[at, :] = jnp.dot(
                p.astype(jnp.bfloat16), v_ref[...], preferred_element_type=jnp.float32
            )

    q1[...] = q0[...]
    l1[...] = l0[...]
    acc1[...] = acc0[...]

    for copy in copies:
        copy.wait()

    off = jnp.int32(0)
    base = 0
    for i in range(n_src):
        tall = talls[i]
        stage = stages[i]
        row = lax.broadcasted_iota(jnp.int32, (tall, HD), 0)
        lane = lanes(tall)
        alive = jnp.where((lane >= 1) & (lane <= 3), 1.0, 0.0).astype(jnp.float32)
        dead = jnp.where(lane == 0, DEAD, 0.0).astype(jnp.float32)

        def pack(j, off, base=base, tall=tall, stage=stage, row=row, alive=alive, dead=dead):
            count = count_ref[base + j]
            at = pl.ds(pl.multiple_of(off, 16), tall)
            kbuf[at, 0:HD] = stage[j, 0:tall, :]
            kbuf[at, HD : 2 * HD] = jnp.where(row < count, alive, dead).astype(jnp.bfloat16)
            vbuf[at, :] = stage[j, tall : 2 * tall, :]
            return off + ((count + 15) // 16) * 16

        off = lax.fori_loop(0, counts[i], pack, off)
        base += counts[i]
    at = pl.ds(pl.multiple_of(off, 16), WIDTH)
    kbuf[at, 0:HD] = jnp.zeros((WIDTH, HD), jnp.bfloat16)
    kbuf[at, HD : 2 * HD] = jnp.where(lanes(WIDTH) == 0, DEAD, 0.0).astype(jnp.bfloat16)
    vbuf[at, :] = jnp.zeros((WIDTH, HD), jnp.bfloat16)
    blocks = (off + WIDTH - 1) // WIDTH

    def block(i, track):
        at = pl.ds(pl.multiple_of(i * WIDTH, WIDTH), WIDTH)
        for t in range(TILES):
            rows = slice(t * TILE, (t + 1) * TILE)
            s = dot_t(q1[rows, :], kbuf[at, :])
            track = jnp.maximum(
                track, jnp.max(by_lanes(jnp.maximum, s).reshape(TILE // 8, 8, HD), axis=0)
            )
            p = jnp.exp2(s * SCALE)
            l1[rows, :] += by_lanes(jnp.add, p)
            acc1[rows, :] += jnp.dot(
                p.astype(jnp.bfloat16), vbuf[at, :], preferred_element_type=jnp.float32
            )
        return track

    track = lax.fori_loop(0, blocks, block, jnp.full((8, HD), DEAD, jnp.float32))

    @pl.when(jnp.max(track) > LIMIT)
    def _():
        for t in range(TILES):
            rows = slice(t * TILE, (t + 1) * TILE)

            def highest(i, top, rows=rows):
                at = pl.ds(pl.multiple_of(i * WIDTH, WIDTH), WIDTH)
                return jnp.maximum(top, by_lanes(jnp.maximum, dot_t(q0[rows, :], kbuf[at, :])))

            top = lax.fori_loop(0, blocks, highest, jnp.zeros((TILE, HD), jnp.float32))
            rise = jnp.max(top, axis=1, keepdims=True)
            columns = q0[rows, HD : 2 * HD].astype(jnp.float32)
            lane = lanes(TILE)
            m = -jnp.sum(
                jnp.where((lane >= 1) & (lane <= 3), columns, 0.0), axis=1, keepdims=True
            )
            factor = jnp.exp2(-rise * SCALE)
            q1[rows, HD : 2 * HD] = reference_columns(m + rise)
            l1[rows, :] = l0[rows, :] * factor
            acc1[rows, :] = acc0[rows, :] * factor
        lax.fori_loop(0, blocks, block, jnp.full((8, HD), DEAD, jnp.float32))

    if last:
        ok = lax.broadcasted_iota(jnp.int32, (CAP, HD), 0) < live
        for h in range(GROUP):
            at = slice(h * CAP, (h + 1) * CAP)
            total = jnp.sum(l1[at, :], axis=1, keepdims=True)
            result = jnp.where(ok, acc1[at, :] / total, 0.0)
            out_ref[:, h * HD : (h + 1) * HD] = result.astype(jnp.bfloat16)


def attention(first, last, count, live, sources, state, interpret=False):
    talls = [ROWS_B if s.shape[1] == TALL_B else ROWS_A for s in sources]
    counts = [s.shape[0] for s in sources]
    keys = sum(c * t for c, t in zip(counts, talls))
    vmem = pl.BlockSpec(memory_space=pltpu.VMEM)
    smem = pl.BlockSpec(memory_space=pltpu.SMEM)
    state_shapes = [
        ((ROWS, 2 * HD), jnp.bfloat16),
        ((ROWS, HD), jnp.float32),
        ((ROWS, HD), jnp.float32),
    ]
    scratch_state = [pltpu.VMEM(*s) for s in state_shapes]
    if last:
        out_shape = jax.ShapeDtypeStruct((CAP, GROUP * HD), jnp.bfloat16)
        out_specs = vmem
    else:
        out_shape = [jax.ShapeDtypeStruct(*s) for s in state_shapes]
        out_specs = [vmem] * 3
    scratch = (
        (scratch_state if last else [])
        + [
            pltpu.VMEM((keys + WIDTH, 2 * HD), jnp.bfloat16),
            pltpu.VMEM((keys + WIDTH, HD), jnp.bfloat16),
            pltpu.SemaphoreType.DMA((len(sources),)),
        ]
        + [pltpu.VMEM(s.shape, jnp.bfloat16) for s in sources]
        + (scratch_state if first else [])
    )

    def kernel(*refs):
        attention_kernel(first, last, talls, counts, *refs)

    return pl.pallas_call(
        kernel,
        out_shape=out_shape,
        in_specs=[smem, smem] + [pl.BlockSpec(memory_space=pl.ANY)] * len(sources) + [vmem] * 3,
        out_specs=out_specs,
        scratch_shapes=scratch,
        compiler_params=pltpu.CompilerParams(vmem_limit_bytes=VMEM_LIMIT),
        cost_estimate=pl.CostEstimate(
            flops=8 * ROWS * keys * HD, bytes_accessed=8 << 20, transcendentals=0
        ),
        interpret=interpret,
    )(count, live, *sources, *state)


def select_kernel(n_src, key_ref, value_ref, *refs):
    sources, (out_ref, pages, sems) = refs[:n_src], refs[n_src:]
    copies = []
    start = 0
    for i, source in enumerate(sources):
        count = source.shape[0]
        copies.append(
            pltpu.make_async_copy(source, pages.at[pl.ds(start, count)], sems.at[i])
        )
        start += count
    for copy in copies:
        copy.start()
    for copy in copies:
        copy.wait()

    def one(s, carry):
        place = key_ref[s]
        keep = jnp.where(place >= 0, 1.0, 0.0).astype(jnp.bfloat16)
        out_ref[s, :, 0:HD] = pages[jnp.maximum(place, 0)] * keep
        out_ref[s, :, HD : 2 * HD] = pages[jnp.maximum(value_ref[s], 0)] * keep
        return carry

    lax.fori_loop(0, 2 * N, one, 0, unroll=4)


def select_pages(key_place, value_place, sources, interpret=False):
    sources = [s.reshape(s.shape[0] * s.shape[1] // PAGE, PAGE, HD) for s in sources]
    total = sum(s.shape[0] for s in sources)
    smem = pl.BlockSpec(memory_space=pltpu.SMEM)

    def kernel(*refs):
        select_kernel(len(sources), *refs)

    return pl.pallas_call(
        kernel,
        out_shape=jax.ShapeDtypeStruct((2 * N, PAGE, 2 * HD), jnp.bfloat16),
        in_specs=[smem, smem] + [pl.BlockSpec(memory_space=pl.ANY)] * len(sources),
        out_specs=pl.BlockSpec(memory_space=pltpu.VMEM),
        scratch_shapes=[
            pltpu.VMEM((total, PAGE, HD), jnp.bfloat16),
            pltpu.SemaphoreType.DMA((len(sources),)),
        ],
        compiler_params=pltpu.CompilerParams(vmem_limit_bytes=VMEM_LIMIT),
        cost_estimate=pl.CostEstimate(flops=0, bytes_accessed=8 << 20, transcendentals=0),
        interpret=interpret,
    )(key_place, value_place, *sources)


def payloads(keys, values, page_owner):
    owner = page_owner[:, 0].astype(jnp.bfloat16)
    owner = jnp.broadcast_to(jnp.pad(owner, (0, HD - PAGES))[None, :], (PAD, HD))
    a = jnp.concatenate([keys[:ROWS_A], values[:ROWS_A], owner], axis=0)
    b = jnp.concatenate([keys[ROWS_A:], values[ROWS_A:]], axis=0)
    return a, b


def layout(me):
    mx, mz = me // NZ, me % NZ
    dx, dz = jnp.array(X_B, jnp.int32), jnp.array(Z_B, jnp.int32)
    piece_b = ((mx + dx + NX) % NX) * NZ + (mz + dz + NZ) % NZ
    dx = jnp.array(X_A * NZ, jnp.int32)
    piece_a = ((mx + dx + NX) % NX) * NZ + jnp.arange(N, dtype=jnp.int32) // NX
    return piece_a, piece_b


def pick(table, index):
    place = jnp.arange(N, dtype=jnp.int32)
    return jnp.sum(jnp.where(index[:, None] == place[None, :], table[None, :], 0), axis=1)


def inverse(index):
    place = jnp.arange(N, dtype=jnp.int32)
    return jnp.sum(jnp.where(index[None, :] == place[:, None], place[None, :], 0), axis=1)


def page_places(me, gathered, piece_a, piece_b, lengths):
    place = jnp.arange(N, dtype=jnp.int32)
    owners = gathered[:, 2 * ROWS_A, :PAGES]
    page = jnp.arange(PAGES, dtype=jnp.int32)[None, :]
    match = owners == me.astype(jnp.bfloat16)
    low = jnp.min(jnp.where(match, page, PAGES), axis=1)
    high = jnp.max(jnp.where(match, page, -1), axis=1)
    pages = jnp.stack([low, jnp.where(high > low, high, PAGES)], axis=1)
    hit = piece_a[None, :] == place[:, None]
    pages = jnp.sum(jnp.where(hit[:, :, None], pages[None, :, :], 0), axis=1)
    at_a = inverse(piece_a)[:, None] * (TALL_A // PAGE) + pages
    at_b = N * (TALL_A // PAGE) + inverse(piece_b)[:, None] * (TALL_B // PAGE) + pages - PAGES_A
    in_a = pages < PAGES_A
    key_place = jnp.where(in_a, at_a, at_b)
    value_place = key_place + jnp.where(in_a, PAGES_A, PAGES_B)
    finished = (pages < PAGES) & ((pages + 1) * PAGE <= lengths[:, None])
    key_place = jnp.where(finished, key_place, -1)
    value_place = jnp.where(finished, value_place, -1)
    return key_place.reshape(2 * N), value_place.reshape(2 * N)


def live_counts(me, lengths, piece_a, piece_b):
    count_a = jnp.where(piece_a < me, jnp.minimum(pick(lengths, piece_a), ROWS_A), 0)
    count_b = jnp.where(piece_b < me, jnp.maximum(pick(lengths, piece_b) - ROWS_A, 0), 0)
    return count_a, count_b


def body(queries, keys, values, lengths, page_owner):
    me = lax.axis_index("ctx")
    live = jnp.sum(jnp.where(jnp.arange(N, dtype=jnp.int32) == me, lengths, 0)).reshape(1)
    gathered, own, beside, across = exchange(*payloads(keys, values, page_owner))
    piece_a, piece_b = layout(me)
    count_a, count_b = live_counts(me, lengths, piece_a, piece_b)
    key_place, value_place = page_places(me, gathered, piece_a, piece_b, lengths)
    outgoing = select_pages(key_place, value_place, [gathered] + own + beside + across)
    decode_cache = lax.all_to_all(
        outgoing.reshape(2 * N, PAGE, 1, 2 * HD), "tp", split_axis=0, concat_axis=2, tiled=True
    )
    state = attention(True, False, count_b[:16], live, own, (queries, keys, values))
    state = attention(False, False, count_b[16:48], live, beside, state)
    attended = attention(
        False, True, jnp.concatenate([count_b[48:], count_a]), live, across + [gathered], state
    )
    return (attended, decode_cache.reshape((1,) + decode_cache.shape))


def solution(mesh):
    in_specs = (P("ctx", "tp"), P("ctx", "tp"), P("ctx", "tp"), P(), P("ctx", None))
    out_specs = (P("ctx", "tp"), P("ctx", "tp", None, None, None))
    return jax.shard_map(body, mesh=mesh, in_specs=in_specs, out_specs=out_specs, check_vma=False)
```

```python
import math

import jax
import jax.numpy as jnp
from jax import lax
from jax.experimental import pallas as pl
from jax.experimental.pallas import tpu as pltpu
from jax.sharding import PartitionSpec as P

HD = 128
PAGE = 2
NX = 4
NZ = 16
N = NX * NZ
CAP = 192
ROWS_A = 48
ROWS_B = CAP - ROWS_A
PAGES = CAP // PAGE
PAGES_A = ROWS_A // PAGE
PAGES_B = ROWS_B // PAGE
PAD = 16
TALL_A = 2 * ROWS_A + PAD
TALL_B = 2 * ROWS_B
GROUP = 8
ROWS = GROUP * CAP
TILES = 4
TILE = ROWS // TILES
WIDTH = 512
DEAD = -1e30
SCALE = math.log2(math.e) / math.sqrt(HD)
LIMIT = 64.0 / SCALE
VMEM_LIMIT = 56 * 1024 * 1024

X_GROUPS = [[x * NZ + z for x in range(NX)] for z in range(NZ)]
Z_GROUPS = [[x * NZ + z for z in range(NZ)] for x in range(NX)]
STEP = 4
STEP_GROUPS = [
    [x * NZ + r + STEP * j for j in range(NZ // STEP)] for x in range(NX) for r in range(STEP)
]
RESIDUES = [0] * 4 + [-1] * 4 + [1] * 4 + [2] * 4


def shift(value, dx, dz):
    pairs = [
        (x * NZ + z, ((x + dx) % NX) * NZ + (z + dz) % NZ) for x in range(NX) for z in range(NZ)
    ]
    return lax.ppermute(value, "ctx", pairs)


def gather_z(value):
    return lax.all_gather(value, "ctx", axis=0, tiled=False, axis_index_groups=Z_GROUPS)


def share(value, groups):
    value = jnp.broadcast_to(value[None], (len(groups[0]),) + value.shape)
    return lax.all_to_all(
        value, "ctx", split_axis=0, concat_axis=0, tiled=True, axis_index_groups=groups
    )


def exchange(a, b):
    gathered = gather_z(share(a, X_GROUPS)).reshape(N, TALL_A, HD)
    first = share(b, STEP_GROUPS)
    own = jnp.concatenate(
        [
            first,
            shift(first, 0, 1),
            shift(first, 0, -1),
            shift(first[:2], 0, 2),
            shift(first[2:], 0, -2),
        ],
        axis=0,
    )
    left, right = shift(own, 1, 0), shift(own, -1, 0)
    far_left, far_right = shift(left[:8], 1, 0), shift(right[8:], -1, 0)
    return gathered, [own], [left, right], [far_left, far_right]


def lanes(rows):
    return lax.broadcasted_iota(jnp.int32, (rows, HD), 1)


def reference_columns(m):
    rows = m.shape[0]
    m = jnp.broadcast_to(m, (rows, HD))
    high = m.astype(jnp.bfloat16).astype(jnp.float32)
    rest = m - high
    middle = rest.astype(jnp.bfloat16).astype(jnp.float32)
    low = rest - middle
    lane = lanes(rows)
    out = jnp.where(lane == 0, 1.0, 0.0)
    out = jnp.where(lane == 1, -high, out)
    out = jnp.where(lane == 2, -middle, out)
    out = jnp.where(lane == 3, -low, out)
    return out.astype(jnp.bfloat16)


def dot_t(a, b):
    return lax.dot_general(a, b, (((1,), (1,)), ((), ())), preferred_element_type=jnp.float32)


def by_lanes(op, s):
    out = s[:, :HD]
    for i in range(1, s.shape[1] // HD):
        out = op(out, s[:, i * HD : (i + 1) * HD])
    return out


def attention_kernel(first, last, talls, counts, *refs):
    n_src = len(talls)
    count_ref, live_ref = refs[0], refs[1]
    sources = refs[2 : 2 + n_src]
    refs = refs[2 + n_src :]
    if first:
        (q_ref, k_ref, v_ref), refs = refs[:3], refs[3:]
    else:
        (q0, l0, acc0), refs = refs[:3], refs[3:]
    if last:
        out_ref, refs = refs[0], refs[1:]
    q1, l1, acc1, kbuf, vbuf, sems = refs[:6]
    stages, refs = refs[6 : 6 + n_src], refs[6 + n_src :]
    if first:
        q0, l0, acc0 = refs
    live = live_ref[0]

    copies = [
        pltpu.make_async_copy(sources[i], stages[i], sems.at[i]) for i in range(n_src)
    ]
    for copy in copies:
        copy.start()

    if first:
        row = lax.broadcasted_iota(jnp.int32, (CAP, CAP), 0)
        col = lax.broadcasted_iota(jnp.int32, (CAP, CAP), 1)
        bias = jnp.where((col <= row) & (col < live), 0.0, DEAD).astype(jnp.float32)
        for h in range(GROUP):
            at = slice(h * CAP, (h + 1) * CAP)
            q = q_ref[:, h * HD : (h + 1) * HD]
            s = dot_t(q, k_ref[...]) + bias
            top = jnp.max(s, axis=1, keepdims=True)
            p = jnp.exp2((s - top) * SCALE)
            q0[at, 0:HD] = q
            q0[at, HD : 2 * HD] = reference_columns(top)
            l0[at, :] = jnp.where(lanes(CAP) == 0, jnp.sum(p, axis=1, keepdims=True), 0.0)
            acc0[at, :] = jnp.dot(
                p.astype(jnp.bfloat16), v_ref[...], preferred_element_type=jnp.float32
            )

    q1[...] = q0[...]
    l1[...] = l0[...]
    acc1[...] = acc0[...]

    for copy in copies:
        copy.wait()

    off = jnp.int32(0)
    base = 0
    for i in range(n_src):
        tall = talls[i]
        stage = stages[i]
        row = lax.broadcasted_iota(jnp.int32, (tall, HD), 0)
        lane = lanes(tall)
        alive = jnp.where((lane >= 1) & (lane <= 3), 1.0, 0.0).astype(jnp.float32)
        dead = jnp.where(lane == 0, DEAD, 0.0).astype(jnp.float32)

        def pack(j, off, base=base, tall=tall, stage=stage, row=row, alive=alive, dead=dead):
            count = count_ref[base + j]
            at = pl.ds(pl.multiple_of(off, 16), tall)
            kbuf[at, 0:HD] = stage[j, 0:tall, :]
            kbuf[at, HD : 2 * HD] = jnp.where(row < count, alive, dead).astype(jnp.bfloat16)
            vbuf[at, :] = stage[j, tall : 2 * tall, :]
            return off + ((count + 15) // 16) * 16

        off = lax.fori_loop(0, counts[i], pack, off)
        base += counts[i]
    at = pl.ds(pl.multiple_of(off, 16), WIDTH)
    kbuf[at, 0:HD] = jnp.zeros((WIDTH, HD), jnp.bfloat16)
    kbuf[at, HD : 2 * HD] = jnp.where(lanes(WIDTH) == 0, DEAD, 0.0).astype(jnp.bfloat16)
    vbuf[at, :] = jnp.zeros((WIDTH, HD), jnp.bfloat16)
    blocks = (off + WIDTH - 1) // WIDTH

    def block(i, track):
        at = pl.ds(pl.multiple_of(i * WIDTH, WIDTH), WIDTH)
        for t in range(TILES):
            rows = slice(t * TILE, (t + 1) * TILE)
            s = dot_t(q1[rows, :], kbuf[at, :])
            track = jnp.maximum(
                track, jnp.max(by_lanes(jnp.maximum, s).reshape(TILE // 8, 8, HD), axis=0)
            )
            p = jnp.exp2(s * SCALE)
            l1[rows, :] += by_lanes(jnp.add, p)
            acc1[rows, :] += jnp.dot(
                p.astype(jnp.bfloat16), vbuf[at, :], preferred_element_type=jnp.float32
            )
        return track

    track = lax.fori_loop(0, blocks, block, jnp.full((8, HD), DEAD, jnp.float32))

    @pl.when(jnp.max(track) > LIMIT)
    def _():
        for t in range(TILES):
            rows = slice(t * TILE, (t + 1) * TILE)

            def highest(i, top, rows=rows):
                at = pl.ds(pl.multiple_of(i * WIDTH, WIDTH), WIDTH)
                return jnp.maximum(top, by_lanes(jnp.maximum, dot_t(q0[rows, :], kbuf[at, :])))

            top = lax.fori_loop(0, blocks, highest, jnp.zeros((TILE, HD), jnp.float32))
            rise = jnp.max(top, axis=1, keepdims=True)
            columns = q0[rows, HD : 2 * HD].astype(jnp.float32)
            lane = lanes(TILE)
            m = -jnp.sum(
                jnp.where((lane >= 1) & (lane <= 3), columns, 0.0), axis=1, keepdims=True
            )
            factor = jnp.exp2(-rise * SCALE)
            q1[rows, HD : 2 * HD] = reference_columns(m + rise)
            l1[rows, :] = l0[rows, :] * factor
            acc1[rows, :] = acc0[rows, :] * factor
        lax.fori_loop(0, blocks, block, jnp.full((8, HD), DEAD, jnp.float32))

    if last:
        ok = lax.broadcasted_iota(jnp.int32, (CAP, HD), 0) < live
        for h in range(GROUP):
            at = slice(h * CAP, (h + 1) * CAP)
            total = jnp.sum(l1[at, :], axis=1, keepdims=True)
            result = jnp.where(ok, acc1[at, :] / total, 0.0)
            out_ref[:, h * HD : (h + 1) * HD] = result.astype(jnp.bfloat16)


def attention(first, last, count, live, sources, state, interpret=False):
    talls = [ROWS_B if s.shape[1] == TALL_B else ROWS_A for s in sources]
    counts = [s.shape[0] for s in sources]
    keys = sum(c * t for c, t in zip(counts, talls))
    vmem = pl.BlockSpec(memory_space=pltpu.VMEM)
    smem = pl.BlockSpec(memory_space=pltpu.SMEM)
    state_shapes = [
        ((ROWS, 2 * HD), jnp.bfloat16),
        ((ROWS, HD), jnp.float32),
        ((ROWS, HD), jnp.float32),
    ]
    scratch_state = [pltpu.VMEM(*s) for s in state_shapes]
    if last:
        out_shape = jax.ShapeDtypeStruct((CAP, GROUP * HD), jnp.bfloat16)
        out_specs = vmem
    else:
        out_shape = [jax.ShapeDtypeStruct(*s) for s in state_shapes]
        out_specs = [vmem] * 3
    scratch = (
        (scratch_state if last else [])
        + [
            pltpu.VMEM((keys + WIDTH, 2 * HD), jnp.bfloat16),
            pltpu.VMEM((keys + WIDTH, HD), jnp.bfloat16),
            pltpu.SemaphoreType.DMA((len(sources),)),
        ]
        + [pltpu.VMEM(s.shape, jnp.bfloat16) for s in sources]
        + (scratch_state if first else [])
    )

    def kernel(*refs):
        attention_kernel(first, last, talls, counts, *refs)

    return pl.pallas_call(
        kernel,
        out_shape=out_shape,
        in_specs=[smem, smem] + [pl.BlockSpec(memory_space=pl.ANY)] * len(sources) + [vmem] * 3,
        out_specs=out_specs,
        scratch_shapes=scratch,
        compiler_params=pltpu.CompilerParams(vmem_limit_bytes=VMEM_LIMIT),
        cost_estimate=pl.CostEstimate(
            flops=8 * ROWS * keys * HD, bytes_accessed=8 << 20, transcendentals=0
        ),
        interpret=interpret,
    )(count, live, *sources, *state)


def run_attention(
    gathered, own, beside, across, count_a, count_b, live, arrays, interpret=False
):
    state = attention(True, False, count_b[:16], live, own, arrays, interpret)
    count = jnp.concatenate([count_b[16:48], count_a])
    state = attention(False, False, count, live, beside + [gathered], state, interpret)
    return attention(False, True, count_b[48:], live, across, state, interpret)


def fetch(sources, pages, sems):
    copies = []
    start = 0
    for i, source in enumerate(sources):
        count = source.shape[0]
        copies.append(
            pltpu.make_async_copy(source, pages.at[pl.ds(start, count)], sems.at[i])
        )
        start += count
    for copy in copies:
        copy.start()
    for copy in copies:
        copy.wait()
    return start


def select_kernel(n_src, key_ref, value_ref, *refs):
    sources, (out_ref, pages, sems) = refs[:n_src], refs[n_src:]
    total = fetch(sources, pages, sems)

    def one(s, carry):
        place = key_ref[s]
        found = (place >= 0) & (place < total)
        keep = jnp.where(found, 1.0, 0.0).astype(jnp.bfloat16)
        key = jnp.where(found, place, 0)
        value = jnp.where(found, value_ref[s], 0)
        out_ref[s, :, 0:HD] = pages[key] * keep
        out_ref[s, :, HD : 2 * HD] = pages[value] * keep
        return carry

    lax.fori_loop(0, 2 * N, one, 0, unroll=4)


def select_rest_kernel(n_src, base, key_ref, value_ref, piece_ref, old_ref, *refs):
    sources, (out_ref, pages, sems) = refs[:n_src], refs[n_src:]
    fetch(sources, pages, sems)
    out_ref[...] = old_ref[...]

    def one(j, carry):
        for r in range(2):
            s = piece_ref[j] * 2 + r
            place = key_ref[s] - base

            @pl.when(place >= 0)
            def _():
                out_ref[s, :, 0:HD] = pages[place]
                out_ref[s, :, HD : 2 * HD] = pages[value_ref[s] - base]

        return carry

    lax.fori_loop(0, 16, one, 0)


def select_call(kernel, scalars, arrays, sources, interpret):
    sources = [s.reshape(s.shape[0] * s.shape[1] // PAGE, PAGE, HD) for s in sources]
    total = sum(s.shape[0] for s in sources)
    smem = pl.BlockSpec(memory_space=pltpu.SMEM)
    vmem = pl.BlockSpec(memory_space=pltpu.VMEM)
    return pl.pallas_call(
        kernel,
        out_shape=jax.ShapeDtypeStruct((2 * N, PAGE, 2 * HD), jnp.bfloat16),
        in_specs=[smem] * len(scalars)
        + [vmem] * len(arrays)
        + [pl.BlockSpec(memory_space=pl.ANY)] * len(sources),
        out_specs=vmem,
        scratch_shapes=[
            pltpu.VMEM((total, PAGE, HD), jnp.bfloat16),
            pltpu.SemaphoreType.DMA((len(sources),)),
        ],
        compiler_params=pltpu.CompilerParams(vmem_limit_bytes=VMEM_LIMIT),
        cost_estimate=pl.CostEstimate(flops=0, bytes_accessed=8 << 20, transcendentals=0),
        interpret=interpret,
    )(*scalars, *arrays, *sources)


def select_pages(key_place, value_place, near, far, piece_far, interpret=False):
    base = sum(s.shape[0] * s.shape[1] // PAGE for s in near)

    def kernel(*refs):
        select_kernel(len(near), *refs)

    def rest_kernel(*refs):
        select_rest_kernel(len(far), base, *refs)

    out = select_call(kernel, (key_place, value_place), (), near, interpret)
    return select_call(
        rest_kernel, (key_place, value_place, piece_far), (out,), far, interpret
    )


def payloads(keys, values, page_owner):
    owner = page_owner[:, 0].astype(jnp.bfloat16)
    owner = jnp.broadcast_to(jnp.pad(owner, (0, HD - PAGES))[None, :], (PAD, HD))
    a = jnp.concatenate([keys[:ROWS_A], values[:ROWS_A], owner], axis=0)
    b = jnp.concatenate([keys[ROWS_A:], values[ROWS_A:]], axis=0)
    return a, b


def layout(me):
    mx, mz = me // NZ, me % NZ
    place = jnp.arange(N, dtype=jnp.int32)
    dx = jnp.array([0] * 16 + [-1] * 16 + [1] * 16 + [2] * 16, jnp.int32)
    residue = (mz + jnp.array(RESIDUES * NX, jnp.int32) + NZ) % STEP
    piece_b = ((mx + dx + NX) % NX) * NZ + residue + STEP * (place % 4)
    piece_a = (place % NX) * NZ + place // NX
    return piece_a, piece_b


def pick(table, index):
    place = jnp.arange(N, dtype=jnp.int32)
    return jnp.sum(jnp.where(index[:, None] == place[None, :], table[None, :], 0), axis=1)


def inverse(index):
    place = jnp.arange(N, dtype=jnp.int32)
    return jnp.sum(jnp.where(index[None, :] == place[:, None], place[None, :], 0), axis=1)


def page_places(me, gathered, piece_a, piece_b, lengths):
    place = jnp.arange(N, dtype=jnp.int32)
    owners = gathered[:, 2 * ROWS_A, :PAGES]
    page = jnp.arange(PAGES, dtype=jnp.int32)[None, :]
    match = owners == me.astype(jnp.bfloat16)
    low = jnp.min(jnp.where(match, page, PAGES), axis=1)
    high = jnp.max(jnp.where(match, page, -1), axis=1)
    pages = jnp.stack([low, jnp.where(high > low, high, PAGES)], axis=1)
    hit = piece_a[None, :] == place[:, None]
    pages = jnp.sum(jnp.where(hit[:, :, None], pages[None, :, :], 0), axis=1)
    at_a = inverse(piece_a)[:, None] * (TALL_A // PAGE) + pages
    at_b = N * (TALL_A // PAGE) + inverse(piece_b)[:, None] * (TALL_B // PAGE) + pages - PAGES_A
    in_a = pages < PAGES_A
    key_place = jnp.where(in_a, at_a, at_b)
    value_place = key_place + jnp.where(in_a, PAGES_A, PAGES_B)
    finished = (pages < PAGES) & ((pages + 1) * PAGE <= lengths[:, None])
    key_place = jnp.where(finished, key_place, -1)
    value_place = jnp.where(finished, value_place, -1)
    return key_place.reshape(2 * N), value_place.reshape(2 * N)


def live_counts(me, lengths, piece_a, piece_b):
    count_a = jnp.where(piece_a < me, jnp.minimum(pick(lengths, piece_a), ROWS_A), 0)
    count_b = jnp.where(piece_b < me, jnp.maximum(pick(lengths, piece_b) - ROWS_A, 0), 0)
    return count_a, count_b


def body(queries, keys, values, lengths, page_owner):
    me = lax.axis_index("ctx")
    live = jnp.sum(jnp.where(jnp.arange(N, dtype=jnp.int32) == me, lengths, 0)).reshape(1)
    gathered, own, beside, across = exchange(*payloads(keys, values, page_owner))
    piece_a, piece_b = layout(me)
    count_a, count_b = live_counts(me, lengths, piece_a, piece_b)
    key_place, value_place = page_places(me, gathered, piece_a, piece_b, lengths)
    outgoing = select_pages(
        key_place, value_place, [gathered] + own + beside, across, piece_b[48:]
    )
    decode_cache = lax.all_to_all(
        outgoing.reshape(2 * N, PAGE, 1, 2 * HD), "tp", split_axis=0, concat_axis=2, tiled=True
    )
    attended = run_attention(
        gathered, own, beside, across, count_a, count_b, live, (queries, keys, values)
    )
    return (attended, decode_cache.reshape((1,) + decode_cache.shape))


def solution(mesh):
    in_specs = (P("ctx", "tp"), P("ctx", "tp"), P("ctx", "tp"), P(), P("ctx", None))
    out_specs = (P("ctx", "tp"), P("ctx", "tp", None, None, None))
    return jax.shard_map(body, mesh=mesh, in_specs=in_specs, out_specs=out_specs, check_vma=False)
```

```python
import math

import jax
import jax.numpy as jnp
from jax import lax
from jax.experimental import pallas as pl
from jax.experimental.pallas import tpu as pltpu
from jax.sharding import PartitionSpec as P

HD = 128
PAGE = 2
NX = 4
NZ = 16
N = NX * NZ
CAP = 192
ROWS_A = 64
ROWS_B = CAP - ROWS_A
PAGES = CAP // PAGE
PAGES_A = ROWS_A // PAGE
PAGES_B = ROWS_B // PAGE
PAD = 16
TALL_A = 2 * ROWS_A + PAD
TALL_B = 2 * ROWS_B
GROUP = 8
ROWS = GROUP * CAP
TILES = 4
TILE = ROWS // TILES
WIDTH = 512
DEAD = -1e30
SCALE = math.log2(math.e) / math.sqrt(HD)
LIMIT = 64.0 / SCALE
VMEM_LIMIT = 56 * 1024 * 1024

X_ORDER = [0, -1, 1, 2]
Z_ORDER = [4, 0, -4, 8]
Z_GROUPS = [[x * NZ + z for z in range(NZ)] for x in range(NX)]
STEP = 4
Z_ALL = [d + s for d in (0, -1, 1) for s in Z_ORDER] + [-2, -6, 6, 2]


def shift(value, dx, dz):
    pairs = [
        (x * NZ + z, ((x + dx) % NX) * NZ + (z + dz) % NZ) for x in range(NX) for z in range(NZ)
    ]
    return lax.ppermute(value, "ctx", pairs)


def gather_z(value):
    return lax.all_gather(value, "ctx", axis=0, tiled=False, axis_index_groups=Z_GROUPS)


def exchange(a, b):
    near = [shift(a, dx, 0) for dx in (1, -1, 2)]
    left, right = shift(b, 0, 4), shift(b, 0, -4)
    gathered = gather_z(jnp.stack([a] + near)).reshape(N, TALL_A, HD)
    far = jnp.concatenate([shift(left[:ROWS_B], 0, 4), shift(right[ROWS_B:], 0, -4)], axis=0)
    first = jnp.stack([right, b, left, far])
    own = jnp.concatenate(
        [
            first,
            shift(first, 0, 1),
            shift(first, 0, -1),
            shift(first[1:3], 0, 2),
            shift(first[:2], 0, -2),
        ],
        axis=0,
    )
    left, right = shift(own, 1, 0), shift(own, -1, 0)
    far_left, far_right = shift(left[:8], 1, 0), shift(right[8:], -1, 0)
    return gathered, [own], [left, right], [far_left, far_right]


def lanes(rows):
    return lax.broadcasted_iota(jnp.int32, (rows, HD), 1)


def reference_columns(m):
    rows = m.shape[0]
    m = jnp.broadcast_to(m, (rows, HD))
    high = m.astype(jnp.bfloat16).astype(jnp.float32)
    rest = m - high
    middle = rest.astype(jnp.bfloat16).astype(jnp.float32)
    low = rest - middle
    lane = lanes(rows)
    out = jnp.where(lane == 0, 1.0, 0.0)
    out = jnp.where(lane == 1, -high, out)
    out = jnp.where(lane == 2, -middle, out)
    out = jnp.where(lane == 3, -low, out)
    return out.astype(jnp.bfloat16)


def dot_t(a, b):
    return lax.dot_general(a, b, (((1,), (1,)), ((), ())), preferred_element_type=jnp.float32)


def by_lanes(op, s):
    out = s[:, :HD]
    for i in range(1, s.shape[1] // HD):
        out = op(out, s[:, i * HD : (i + 1) * HD])
    return out


def attention_kernel(first, last, talls, counts, *refs):
    n_src = len(talls)
    count_ref, live_ref = refs[0], refs[1]
    sources = refs[2 : 2 + n_src]
    refs = refs[2 + n_src :]
    if first:
        (q_ref, k_ref, v_ref), refs = refs[:3], refs[3:]
    else:
        (q0, l0, acc0), refs = refs[:3], refs[3:]
    if last:
        out_ref, refs = refs[0], refs[1:]
    q1, l1, acc1, kbuf, vbuf, sems = refs[:6]
    stages, refs = refs[6 : 6 + n_src], refs[6 + n_src :]
    if first:
        q0, l0, acc0 = refs
    live = live_ref[0]

    copies = [
        pltpu.make_async_copy(sources[i], stages[i], sems.at[i]) for i in range(n_src)
    ]
    for copy in copies:
        copy.start()

    if first:
        row = lax.broadcasted_iota(jnp.int32, (CAP, CAP), 0)
        col = lax.broadcasted_iota(jnp.int32, (CAP, CAP), 1)
        bias = jnp.where((col <= row) & (col < live), 0.0, DEAD).astype(jnp.float32)
        for h in range(GROUP):
            at = slice(h * CAP, (h + 1) * CAP)
            q = q_ref[:, h * HD : (h + 1) * HD]
            s = dot_t(q, k_ref[...]) + bias
            top = jnp.max(s, axis=1, keepdims=True)
            p = jnp.exp2((s - top) * SCALE)
            q0[at, 0:HD] = q
            q0[at, HD : 2 * HD] = reference_columns(top)
            l0[at, :] = jnp.where(lanes(CAP) == 0, jnp.sum(p, axis=1, keepdims=True), 0.0)
            acc0[at, :] = jnp.dot(
                p.astype(jnp.bfloat16), v_ref[...], preferred_element_type=jnp.float32
            )

    q1[...] = q0[...]
    l1[...] = l0[...]
    acc1[...] = acc0[...]

    for copy in copies:
        copy.wait()

    off = jnp.int32(0)
    base = 0
    for i in range(n_src):
        tall = talls[i]
        stage = stages[i]
        row = lax.broadcasted_iota(jnp.int32, (tall, HD), 0)
        lane = lanes(tall)
        alive = jnp.where((lane >= 1) & (lane <= 3), 1.0, 0.0).astype(jnp.float32)
        dead = jnp.where(lane == 0, DEAD, 0.0).astype(jnp.float32)

        def pack(j, off, base=base, tall=tall, stage=stage, row=row, alive=alive, dead=dead):
            count = count_ref[base + j]
            at = pl.ds(pl.multiple_of(off, 16), tall)
            kbuf[at, 0:HD] = stage[j, 0:tall, :]
            kbuf[at, HD : 2 * HD] = jnp.where(row < count, alive, dead).astype(jnp.bfloat16)
            vbuf[at, :] = stage[j, tall : 2 * tall, :]
            return off + ((count + 15) // 16) * 16

        off = lax.fori_loop(0, counts[i], pack, off)
        base += counts[i]
    at = pl.ds(pl.multiple_of(off, 16), WIDTH)
    kbuf[at, 0:HD] = jnp.zeros((WIDTH, HD), jnp.bfloat16)
    kbuf[at, HD : 2 * HD] = jnp.where(lanes(WIDTH) == 0, DEAD, 0.0).astype(jnp.bfloat16)
    vbuf[at, :] = jnp.zeros((WIDTH, HD), jnp.bfloat16)
    blocks = (off + WIDTH - 1) // WIDTH

    def block(i, track):
        at = pl.ds(pl.multiple_of(i * WIDTH, WIDTH), WIDTH)
        for t in range(TILES):
            rows = slice(t * TILE, (t + 1) * TILE)
            s = dot_t(q1[rows, :], kbuf[at, :])
            track = jnp.maximum(
                track, jnp.max(by_lanes(jnp.maximum, s).reshape(TILE // 8, 8, HD), axis=0)
            )
            p = jnp.exp2(s * SCALE)
            l1[rows, :] += by_lanes(jnp.add, p)
            acc1[rows, :] += jnp.dot(
                p.astype(jnp.bfloat16), vbuf[at, :], preferred_element_type=jnp.float32
            )
        return track

    track = lax.fori_loop(0, blocks, block, jnp.full((8, HD), DEAD, jnp.float32))

    @pl.when(jnp.max(track) > LIMIT)
    def _():
        for t in range(TILES):
            rows = slice(t * TILE, (t + 1) * TILE)

            def highest(i, top, rows=rows):
                at = pl.ds(pl.multiple_of(i * WIDTH, WIDTH), WIDTH)
                return jnp.maximum(top, by_lanes(jnp.maximum, dot_t(q0[rows, :], kbuf[at, :])))

            top = lax.fori_loop(0, blocks, highest, jnp.zeros((TILE, HD), jnp.float32))
            rise = jnp.max(top, axis=1, keepdims=True)
            columns = q0[rows, HD : 2 * HD].astype(jnp.float32)
            lane = lanes(TILE)
            m = -jnp.sum(
                jnp.where((lane >= 1) & (lane <= 3), columns, 0.0), axis=1, keepdims=True
            )
            factor = jnp.exp2(-rise * SCALE)
            q1[rows, HD : 2 * HD] = reference_columns(m + rise)
            l1[rows, :] = l0[rows, :] * factor
            acc1[rows, :] = acc0[rows, :] * factor
        lax.fori_loop(0, blocks, block, jnp.full((8, HD), DEAD, jnp.float32))

    if last:
        ok = lax.broadcasted_iota(jnp.int32, (CAP, HD), 0) < live
        for h in range(GROUP):
            at = slice(h * CAP, (h + 1) * CAP)
            total = jnp.sum(l1[at, :], axis=1, keepdims=True)
            result = jnp.where(ok, acc1[at, :] / total, 0.0)
            out_ref[:, h * HD : (h + 1) * HD] = result.astype(jnp.bfloat16)


def attention(first, last, count, live, sources, state, interpret=False):
    talls = [ROWS_B if s.shape[1] == TALL_B else ROWS_A for s in sources]
    counts = [s.shape[0] for s in sources]
    keys = sum(c * t for c, t in zip(counts, talls))
    vmem = pl.BlockSpec(memory_space=pltpu.VMEM)
    smem = pl.BlockSpec(memory_space=pltpu.SMEM)
    state_shapes = [
        ((ROWS, 2 * HD), jnp.bfloat16),
        ((ROWS, HD), jnp.float32),
        ((ROWS, HD), jnp.float32),
    ]
    scratch_state = [pltpu.VMEM(*s) for s in state_shapes]
    if last:
        out_shape = jax.ShapeDtypeStruct((CAP, GROUP * HD), jnp.bfloat16)
        out_specs = vmem
    else:
        out_shape = [jax.ShapeDtypeStruct(*s) for s in state_shapes]
        out_specs = [vmem] * 3
    scratch = (
        (scratch_state if last else [])
        + [
            pltpu.VMEM((keys + WIDTH, 2 * HD), jnp.bfloat16),
            pltpu.VMEM((keys + WIDTH, HD), jnp.bfloat16),
            pltpu.SemaphoreType.DMA((len(sources),)),
        ]
        + [pltpu.VMEM(s.shape, jnp.bfloat16) for s in sources]
        + (scratch_state if first else [])
    )

    def kernel(*refs):
        attention_kernel(first, last, talls, counts, *refs)

    return pl.pallas_call(
        kernel,
        out_shape=out_shape,
        in_specs=[smem, smem] + [pl.BlockSpec(memory_space=pl.ANY)] * len(sources) + [vmem] * 3,
        out_specs=out_specs,
        scratch_shapes=scratch,
        compiler_params=pltpu.CompilerParams(vmem_limit_bytes=VMEM_LIMIT),
        cost_estimate=pl.CostEstimate(
            flops=8 * ROWS * keys * HD, bytes_accessed=8 << 20, transcendentals=0
        ),
        interpret=interpret,
    )(count, live, *sources, *state)


def early_attention(gathered, own, beside, count_a, count_b, live, arrays, interpret=False):
    state = attention(True, False, count_b[:16], live, own, arrays, interpret)
    state = attention(False, False, count_b[16:48], live, beside, state, interpret)
    return attention(False, False, count_a, live, [gathered], state, interpret)


def late_attention(across, count_b, live, state, interpret=False):
    return attention(False, True, count_b[48:], live, across, state, interpret)


def fetch(sources, pages, sems):
    copies = []
    start = 0
    for i, source in enumerate(sources):
        count = source.shape[0]
        copies.append(
            pltpu.make_async_copy(source, pages.at[pl.ds(start, count)], sems.at[i])
        )
        start += count
    for copy in copies:
        copy.start()
    for copy in copies:
        copy.wait()
    return start


def select_kernel(n_src, key_ref, value_ref, *refs):
    sources, (out_ref, pages, sems) = refs[:n_src], refs[n_src:]
    total = fetch(sources, pages, sems)

    def one(s, carry):
        place = key_ref[s]
        found = (place >= 0) & (place < total)
        keep = jnp.where(found, 1.0, 0.0).astype(jnp.bfloat16)
        key = jnp.where(found, place, 0)
        value = jnp.where(found, value_ref[s], 0)
        out_ref[s, :, 0:HD] = pages[key] * keep
        out_ref[s, :, HD : 2 * HD] = pages[value] * keep
        return carry

    lax.fori_loop(0, 2 * N, one, 0, unroll=4)


def select_rest_kernel(n_src, base, key_ref, value_ref, old_ref, after_ref, *refs):
    sources, (out_ref, pages, sems) = refs[:n_src], refs[n_src:]
    fetch(sources, pages, sems)
    out_ref[...] = old_ref[...]

    def one(s, carry):
        place = key_ref[s] - base

        @pl.when(place >= 0)
        def _():
            out_ref[s, :, 0:HD] = pages[place]
            out_ref[s, :, HD : 2 * HD] = pages[value_ref[s] - base]

        return carry

    lax.fori_loop(0, 2 * N, one, 0, unroll=2)


def select_call(kernel, scalars, arrays, sources, interpret):
    total = sum(s.shape[0] for s in sources)
    smem = pl.BlockSpec(memory_space=pltpu.SMEM)
    vmem = pl.BlockSpec(memory_space=pltpu.VMEM)
    anywhere = pl.BlockSpec(memory_space=pl.ANY)
    return pl.pallas_call(
        kernel,
        out_shape=jax.ShapeDtypeStruct((2 * N, PAGE, 2 * HD), jnp.bfloat16),
        in_specs=[smem] * len(scalars)
        + [vmem, anywhere][: len(arrays)]
        + [anywhere] * len(sources),
        out_specs=vmem,
        scratch_shapes=[
            pltpu.VMEM((total, PAGE, HD), jnp.bfloat16),
            pltpu.SemaphoreType.DMA((len(sources),)),
        ],
        compiler_params=pltpu.CompilerParams(vmem_limit_bytes=VMEM_LIMIT),
        cost_estimate=pl.CostEstimate(flops=0, bytes_accessed=4 << 20, transcendentals=0),
        interpret=interpret,
    )(*scalars, *arrays, *sources)


def as_pages(sources):
    return [s.reshape(s.shape[0] * s.shape[1] // PAGE, PAGE, HD) for s in sources]


def select_pages(places, near, rest, after, interpret=False):
    near, rest = as_pages(near), as_pages(rest)
    base = sum(s.shape[0] for s in near)

    def kernel(*refs):
        select_kernel(len(near), *refs)

    def rest_kernel(*refs):
        select_rest_kernel(len(rest), base, *refs)

    out = select_call(kernel, places, (), near, interpret)
    return select_call(rest_kernel, places, (out, after), rest, interpret)


def payload_kernel(k_ref, v_ref, owner_ref, a_ref, b_ref):
    a_ref[0:ROWS_A, :] = k_ref[0:ROWS_A, :]
    a_ref[ROWS_A : 2 * ROWS_A, :] = v_ref[0:ROWS_A, :]
    a_ref[2 * ROWS_A :, :] = jnp.zeros((PAD, HD), jnp.bfloat16)
    owner = jnp.broadcast_to(owner_ref[...].astype(jnp.float32), (PAD, PAGES))
    a_ref[2 * ROWS_A :, 0:PAGES] = owner.astype(jnp.bfloat16)
    b_ref[0:ROWS_B, :] = k_ref[ROWS_A:, :]
    b_ref[ROWS_B:, :] = v_ref[ROWS_A:, :]


def payloads(keys, values, page_owner, interpret=False):
    vmem = pl.BlockSpec(memory_space=pltpu.VMEM)
    return pl.pallas_call(
        payload_kernel,
        out_shape=[
            jax.ShapeDtypeStruct((TALL_A, HD), jnp.bfloat16),
            jax.ShapeDtypeStruct((TALL_B, HD), jnp.bfloat16),
        ],
        in_specs=[vmem] * 3,
        out_specs=[vmem] * 2,
        interpret=interpret,
    )(keys, values, page_owner.reshape(1, PAGES))


def layout(me):
    mx, mz = me // NZ, me % NZ
    dx = jnp.array([0] * 16 + [-1] * 16 + [1] * 16 + [2] * 16, jnp.int32)
    dz = jnp.array(Z_ALL * NX, jnp.int32)
    piece_b = ((mx + dx + NX) % NX) * NZ + (mz + dz + NZ) % NZ
    dx = jnp.array(X_ORDER * NZ, jnp.int32)
    piece_a = ((mx + dx + NX) % NX) * NZ + jnp.arange(N, dtype=jnp.int32) // NX
    return piece_a, piece_b


def pick(table, index):
    place = jnp.arange(N, dtype=jnp.int32)
    return jnp.sum(jnp.where(index[:, None] == place[None, :], table[None, :], 0), axis=1)


def inverse(index):
    place = jnp.arange(N, dtype=jnp.int32)
    return jnp.sum(jnp.where(index[None, :] == place[:, None], place[None, :], 0), axis=1)


def page_places(me, gathered, piece_a, piece_b, lengths):
    place = jnp.arange(N, dtype=jnp.int32)
    owners = gathered[:, 2 * ROWS_A, :PAGES]
    page = jnp.arange(PAGES, dtype=jnp.int32)[None, :]
    match = owners == me.astype(jnp.bfloat16)
    low = jnp.min(jnp.where(match, page, PAGES), axis=1)
    high = jnp.max(jnp.where(match, page, -1), axis=1)
    pages = jnp.stack([low, jnp.where(high > low, high, PAGES)], axis=1)
    hit = piece_a[None, :] == place[:, None]
    pages = jnp.sum(jnp.where(hit[:, :, None], pages[None, :, :], 0), axis=1)
    at_a = N * (TALL_B // PAGE) + inverse(piece_a)[:, None] * (TALL_A // PAGE) + pages
    at_b = inverse(piece_b)[:, None] * (TALL_B // PAGE) + pages - PAGES_A
    in_a = pages < PAGES_A
    key_place = jnp.where(in_a, at_a, at_b)
    value_place = key_place + jnp.where(in_a, PAGES_A, PAGES_B)
    finished = (pages < PAGES) & ((pages + 1) * PAGE <= lengths[:, None])
    key_place = jnp.where(finished, key_place, -1)
    value_place = jnp.where(finished, value_place, -1)
    return key_place.reshape(2 * N), value_place.reshape(2 * N)


def live_counts(me, lengths, piece_a, piece_b):
    count_a = jnp.where(piece_a < me, jnp.minimum(pick(lengths, piece_a), ROWS_A), 0)
    count_b = jnp.where(piece_b < me, jnp.maximum(pick(lengths, piece_b) - ROWS_A, 0), 0)
    return count_a, count_b


def body(queries, keys, values, lengths, page_owner):
    me = lax.axis_index("ctx")
    live = jnp.sum(jnp.where(jnp.arange(N, dtype=jnp.int32) == me, lengths, 0)).reshape(1)
    gathered, own, beside, across = exchange(*payloads(keys, values, page_owner))
    piece_a, piece_b = layout(me)
    count_a, count_b = live_counts(me, lengths, piece_a, piece_b)
    key_place, value_place = page_places(me, gathered, piece_a, piece_b, lengths)
    state = early_attention(
        gathered, own, beside, count_a, count_b, live, (queries, keys, values)
    )
    outgoing = select_pages(
        (key_place, value_place), own + beside, across + [gathered], state[1]
    )
    decode_cache = lax.all_to_all(
        outgoing.reshape(2 * N, PAGE, 1, 2 * HD), "tp", split_axis=0, concat_axis=2, tiled=True
    )
    attended = late_attention(across, count_b, live, state)
    return (attended, decode_cache.reshape((1,) + decode_cache.shape))


def solution(mesh):
    in_specs = (P("ctx", "tp"), P("ctx", "tp"), P("ctx", "tp"), P(), P("ctx", None))
    out_specs = (P("ctx", "tp"), P("ctx", "tp", None, None, None))
    return jax.shard_map(body, mesh=mesh, in_specs=in_specs, out_specs=out_specs, check_vma=False)
```

```python
import math

import jax
import jax.numpy as jnp
from jax import lax
from jax.experimental import pallas as pl
from jax.experimental.pallas import tpu as pltpu
from jax.sharding import PartitionSpec as P

HD = 128
PAGE = 2
NX = 4
NZ = 16
N = NX * NZ
CAP = 192
ROWS_A = 96
ROWS_B = CAP - ROWS_A
PAGES = CAP // PAGE
PAGES_A = ROWS_A // PAGE
PAGES_B = ROWS_B // PAGE
PAD = 16
TALL_A = 2 * ROWS_A + PAD
TALL_B = 2 * ROWS_B
GROUP = 8
ROWS = GROUP * CAP
TILES = 2
TILE = ROWS // TILES
WIDTH = 512
DEAD = -1e30
SCALE = math.log2(math.e) / math.sqrt(HD)
LIMIT = 64.0 / SCALE
VMEM_LIMIT = 56 * 1024 * 1024

X_ORDER = [0, -1, 1, 2]
Z_ORDER = [4, 0, -4, 8]
Z_GROUPS = [[x * NZ + z for z in range(NZ)] for x in range(NX)]
STEP = 4
Z_ALL = [d + s for d in (0, -1, 1) for s in Z_ORDER] + [-2, -6, 6, 2]


def shift(value, dx, dz):
    pairs = [
        (x * NZ + z, ((x + dx) % NX) * NZ + (z + dz) % NZ) for x in range(NX) for z in range(NZ)
    ]
    return lax.ppermute(value, "ctx", pairs)


def gather_z(value):
    return lax.all_gather(value, "ctx", axis=0, tiled=False, axis_index_groups=Z_GROUPS)


def exchange(a, b):
    near = [shift(a, dx, 0) for dx in (1, -1, 2)]
    left, right = shift(b, 0, 4), shift(b, 0, -4)
    gathered = gather_z(jnp.stack([a] + near)).reshape(N, TALL_A, HD)
    far = jnp.concatenate([shift(left[:ROWS_B], 0, 4), shift(right[ROWS_B:], 0, -4)], axis=0)
    first = jnp.stack([right, b, left, far])
    own = jnp.concatenate(
        [
            first,
            shift(first, 0, 1),
            shift(first, 0, -1),
            shift(first[1:3], 0, 2),
            shift(first[:2], 0, -2),
        ],
        axis=0,
    )
    left, right = shift(own, 1, 0), shift(own, -1, 0)
    far_left, far_right = shift(left[:8], 1, 0), shift(right[8:], -1, 0)
    return gathered, [own], [left, right], [far_left, far_right]


def lanes(rows):
    return lax.broadcasted_iota(jnp.int32, (rows, HD), 1)


def reference_columns(m):
    rows = m.shape[0]
    m = jnp.broadcast_to(m, (rows, HD))
    high = m.astype(jnp.bfloat16).astype(jnp.float32)
    rest = m - high
    middle = rest.astype(jnp.bfloat16).astype(jnp.float32)
    low = rest - middle
    lane = lanes(rows)
    out = jnp.where(lane == 0, 1.0, 0.0)
    out = jnp.where(lane == 1, -high, out)
    out = jnp.where(lane == 2, -middle, out)
    out = jnp.where(lane == 3, -low, out)
    return out.astype(jnp.bfloat16)


def dot_t(a, b):
    return lax.dot_general(a, b, (((1,), (1,)), ((), ())), preferred_element_type=jnp.float32)


def by_lanes(op, s):
    out = s[:, :HD]
    for i in range(1, s.shape[1] // HD):
        out = op(out, s[:, i * HD : (i + 1) * HD])
    return out


def attention_kernel(first, last, talls, counts, *refs):
    n_src = len(talls)
    count_ref, live_ref = refs[0], refs[1]
    sources = refs[2 : 2 + n_src]
    refs = refs[2 + n_src :]
    if first:
        (q_ref, k_ref, v_ref), refs = refs[:3], refs[3:]
    else:
        (q0, l0, acc0), refs = refs[:3], refs[3:]
    if last:
        out_ref, refs = refs[0], refs[1:]
    q1, l1, acc1, kbuf, vbuf, sems = refs[:6]
    stages, refs = refs[6 : 6 + n_src], refs[6 + n_src :]
    if first:
        q0, l0, acc0 = refs
    live = live_ref[0]

    copies = [
        pltpu.make_async_copy(sources[i], stages[i], sems.at[i]) for i in range(n_src)
    ]
    for copy in copies:
        copy.start()

    if first:
        row = lax.broadcasted_iota(jnp.int32, (CAP, CAP), 0)
        col = lax.broadcasted_iota(jnp.int32, (CAP, CAP), 1)
        bias = jnp.where((col <= row) & (col < live), 0.0, DEAD).astype(jnp.float32)
        for h in range(GROUP):
            at = slice(h * CAP, (h + 1) * CAP)
            q = q_ref[:, h * HD : (h + 1) * HD]
            s = dot_t(q, k_ref[...]) + bias
            top = jnp.max(s, axis=1, keepdims=True)
            p = jnp.exp2((s - top) * SCALE)
            q0[at, 0:HD] = q
            q0[at, HD : 2 * HD] = reference_columns(top)
            l0[at, :] = jnp.where(lanes(CAP) == 0, jnp.sum(p, axis=1, keepdims=True), 0.0)
            acc0[at, :] = jnp.dot(
                p.astype(jnp.bfloat16), v_ref[...], preferred_element_type=jnp.float32
            )

    q1[...] = q0[...]
    l1[...] = l0[...]
    acc1[...] = acc0[...]

    for copy in copies:
        copy.wait()

    off = jnp.int32(0)
    base = 0
    for i in range(n_src):
        tall = talls[i]
        stage = stages[i]
        row = lax.broadcasted_iota(jnp.int32, (tall, HD), 0)
        lane = lanes(tall)
        alive = jnp.where((lane >= 1) & (lane <= 3), 1.0, 0.0).astype(jnp.float32)
        dead = jnp.where(lane == 0, DEAD, 0.0).astype(jnp.float32)

        def pack(j, off, base=base, tall=tall, stage=stage, row=row, alive=alive, dead=dead):
            count = count_ref[base + j]
            at = pl.ds(pl.multiple_of(off, 16), tall)
            kbuf[at, 0:HD] = stage[j, 0:tall, :]
            kbuf[at, HD : 2 * HD] = jnp.where(row < count, alive, dead).astype(jnp.bfloat16)
            vbuf[at, :] = stage[j, tall : 2 * tall, :]
            return off + ((count + 15) // 16) * 16

        off = lax.fori_loop(0, counts[i], pack, off)
        base += counts[i]
    at = pl.ds(pl.multiple_of(off, 16), WIDTH)
    kbuf[at, 0:HD] = jnp.zeros((WIDTH, HD), jnp.bfloat16)
    kbuf[at, HD : 2 * HD] = jnp.where(lanes(WIDTH) == 0, DEAD, 0.0).astype(jnp.bfloat16)
    vbuf[at, :] = jnp.zeros((WIDTH, HD), jnp.bfloat16)
    blocks = (off + WIDTH - 1) // WIDTH

    def block(i, track):
        at = pl.ds(pl.multiple_of(i * WIDTH, WIDTH), WIDTH)
        for t in range(TILES):
            rows = slice(t * TILE, (t + 1) * TILE)
            s = dot_t(q1[rows, :], kbuf[at, :])
            track = jnp.maximum(
                track, jnp.max(by_lanes(jnp.maximum, s).reshape(TILE // 8, 8, HD), axis=0)
            )
            p = jnp.exp2(s * SCALE)
            l1[rows, :] += by_lanes(jnp.add, p)
            acc1[rows, :] += jnp.dot(
                p.astype(jnp.bfloat16), vbuf[at, :], preferred_element_type=jnp.float32
            )
        return track

    track = lax.fori_loop(0, blocks, block, jnp.full((8, HD), DEAD, jnp.float32))

    @pl.when(jnp.max(track) > LIMIT)
    def _():
        for t in range(TILES):
            rows = slice(t * TILE, (t + 1) * TILE)

            def highest(i, top, rows=rows):
                at = pl.ds(pl.multiple_of(i * WIDTH, WIDTH), WIDTH)
                return jnp.maximum(top, by_lanes(jnp.maximum, dot_t(q0[rows, :], kbuf[at, :])))

            top = lax.fori_loop(0, blocks, highest, jnp.zeros((TILE, HD), jnp.float32))
            rise = jnp.max(top, axis=1, keepdims=True)
            columns = q0[rows, HD : 2 * HD].astype(jnp.float32)
            lane = lanes(TILE)
            m = -jnp.sum(
                jnp.where((lane >= 1) & (lane <= 3), columns, 0.0), axis=1, keepdims=True
            )
            factor = jnp.exp2(-rise * SCALE)
            q1[rows, HD : 2 * HD] = reference_columns(m + rise)
            l1[rows, :] = l0[rows, :] * factor
            acc1[rows, :] = acc0[rows, :] * factor
        lax.fori_loop(0, blocks, block, jnp.full((8, HD), DEAD, jnp.float32))

    if last:
        ok = lax.broadcasted_iota(jnp.int32, (CAP, HD), 0) < live
        for h in range(GROUP):
            at = slice(h * CAP, (h + 1) * CAP)
            total = jnp.sum(l1[at, :], axis=1, keepdims=True)
            result = jnp.where(ok, acc1[at, :] / total, 0.0)
            out_ref[:, h * HD : (h + 1) * HD] = result.astype(jnp.bfloat16)


def attention(first, last, count, live, sources, state, interpret=False):
    talls = [ROWS_B if s.shape[1] == TALL_B else ROWS_A for s in sources]
    counts = [s.shape[0] for s in sources]
    keys = sum(c * t for c, t in zip(counts, talls))
    vmem = pl.BlockSpec(memory_space=pltpu.VMEM)
    smem = pl.BlockSpec(memory_space=pltpu.SMEM)
    state_shapes = [
        ((ROWS, 2 * HD), jnp.bfloat16),
        ((ROWS, HD), jnp.float32),
        ((ROWS, HD), jnp.float32),
    ]
    scratch_state = [pltpu.VMEM(*s) for s in state_shapes]
    if last:
        out_shape = jax.ShapeDtypeStruct((CAP, GROUP * HD), jnp.bfloat16)
        out_specs = vmem
    else:
        out_shape = [jax.ShapeDtypeStruct(*s) for s in state_shapes]
        out_specs = [vmem] * 3
    scratch = (
        (scratch_state if last else [])
        + [
            pltpu.VMEM((keys + WIDTH, 2 * HD), jnp.bfloat16),
            pltpu.VMEM((keys + WIDTH, HD), jnp.bfloat16),
            pltpu.SemaphoreType.DMA((len(sources),)),
        ]
        + [pltpu.VMEM(s.shape, jnp.bfloat16) for s in sources]
        + (scratch_state if first else [])
    )

    def kernel(*refs):
        attention_kernel(first, last, talls, counts, *refs)

    return pl.pallas_call(
        kernel,
        out_shape=out_shape,
        in_specs=[smem, smem] + [pl.BlockSpec(memory_space=pl.ANY)] * len(sources) + [vmem] * 3,
        out_specs=out_specs,
        scratch_shapes=scratch,
        compiler_params=pltpu.CompilerParams(vmem_limit_bytes=VMEM_LIMIT),
        cost_estimate=pl.CostEstimate(
            flops=8 * ROWS * keys * HD, bytes_accessed=8 << 20, transcendentals=0
        ),
        interpret=interpret,
    )(count, live, *sources, *state)


def early_attention(own, beside, count_b, live, arrays, interpret=False):
    state = attention(True, False, count_b[:16], live, own, arrays, interpret)
    return attention(False, False, count_b[16:48], live, beside, state, interpret)


def late_attention(gathered, across, count_a, count_b, live, state, interpret=False):
    count = jnp.concatenate([count_b[48:], count_a])
    return attention(False, True, count, live, across + [gathered], state, interpret)


def select_kernel(n_src, key_ref, value_ref, after_ref, *refs):
    sources, (out_ref, pages, sems) = refs[:n_src], refs[n_src:]
    copies = []
    start = 0
    for i, source in enumerate(sources):
        count = source.shape[0]
        copies.append(
            pltpu.make_async_copy(source, pages.at[pl.ds(start, count)], sems.at[i])
        )
        start += count
    for copy in copies:
        copy.start()
    for copy in copies:
        copy.wait()

    def one(s, carry):
        place = key_ref[s]
        keep = jnp.where(place >= 0, 1.0, 0.0).astype(jnp.bfloat16)
        out_ref[s, :, 0:HD] = pages[jnp.maximum(place, 0)] * keep
        out_ref[s, :, HD : 2 * HD] = pages[jnp.maximum(value_ref[s], 0)] * keep
        return carry

    lax.fori_loop(0, 2 * N, one, 0, unroll=4)


def select_pages(places, sources, after, interpret=False):
    sources = [s.reshape(s.shape[0] * s.shape[1] // PAGE, PAGE, HD) for s in sources]
    total = sum(s.shape[0] for s in sources)
    smem = pl.BlockSpec(memory_space=pltpu.SMEM)
    anywhere = pl.BlockSpec(memory_space=pl.ANY)

    def kernel(*refs):
        select_kernel(len(sources), *refs)

    return pl.pallas_call(
        kernel,
        out_shape=jax.ShapeDtypeStruct((2 * N, PAGE, 2 * HD), jnp.bfloat16),
        in_specs=[smem] * 2 + [anywhere] * (1 + len(sources)),
        out_specs=pl.BlockSpec(memory_space=pltpu.VMEM),
        scratch_shapes=[
            pltpu.VMEM((total, PAGE, HD), jnp.bfloat16),
            pltpu.SemaphoreType.DMA((len(sources),)),
        ],
        compiler_params=pltpu.CompilerParams(vmem_limit_bytes=VMEM_LIMIT),
        cost_estimate=pl.CostEstimate(flops=0, bytes_accessed=8 << 20, transcendentals=0),
        interpret=interpret,
    )(*places, after, *sources)


def payload_kernel(k_ref, v_ref, owner_ref, a_ref, b_ref):
    a_ref[0:ROWS_A, :] = k_ref[0:ROWS_A, :]
    a_ref[ROWS_A : 2 * ROWS_A, :] = v_ref[0:ROWS_A, :]
    a_ref[2 * ROWS_A :, :] = jnp.zeros((PAD, HD), jnp.bfloat16)
    owner = jnp.broadcast_to(owner_ref[...].astype(jnp.float32), (PAD, PAGES))
    a_ref[2 * ROWS_A :, 0:PAGES] = owner.astype(jnp.bfloat16)
    b_ref[0:ROWS_B, :] = k_ref[ROWS_A:, :]
    b_ref[ROWS_B:, :] = v_ref[ROWS_A:, :]


def payloads(keys, values, page_owner, interpret=False):
    vmem = pl.BlockSpec(memory_space=pltpu.VMEM)
    return pl.pallas_call(
        payload_kernel,
        out_shape=[
            jax.ShapeDtypeStruct((TALL_A, HD), jnp.bfloat16),
            jax.ShapeDtypeStruct((TALL_B, HD), jnp.bfloat16),
        ],
        in_specs=[vmem] * 3,
        out_specs=[vmem] * 2,
        interpret=interpret,
    )(keys, values, page_owner.reshape(1, PAGES))


def layout(me):
    mx, mz = me // NZ, me % NZ
    dx = jnp.array([0] * 16 + [-1] * 16 + [1] * 16 + [2] * 16, jnp.int32)
    dz = jnp.array(Z_ALL * NX, jnp.int32)
    piece_b = ((mx + dx + NX) % NX) * NZ + (mz + dz + NZ) % NZ
    dx = jnp.array(X_ORDER * NZ, jnp.int32)
    piece_a = ((mx + dx + NX) % NX) * NZ + jnp.arange(N, dtype=jnp.int32) // NX
    return piece_a, piece_b


def pick(table, index):
    place = jnp.arange(N, dtype=jnp.int32)
    return jnp.sum(jnp.where(index[:, None] == place[None, :], table[None, :], 0), axis=1)


def inverse(index):
    place = jnp.arange(N, dtype=jnp.int32)
    return jnp.sum(jnp.where(index[None, :] == place[:, None], place[None, :], 0), axis=1)


def page_places(me, gathered, piece_a, piece_b, lengths):
    place = jnp.arange(N, dtype=jnp.int32)
    owners = gathered[:, 2 * ROWS_A, :PAGES]
    page = jnp.arange(PAGES, dtype=jnp.int32)[None, :]
    match = owners == me.astype(jnp.bfloat16)
    low = jnp.min(jnp.where(match, page, PAGES), axis=1)
    high = jnp.max(jnp.where(match, page, -1), axis=1)
    pages = jnp.stack([low, jnp.where(high > low, high, PAGES)], axis=1)
    hit = piece_a[None, :] == place[:, None]
    pages = jnp.sum(jnp.where(hit[:, :, None], pages[None, :, :], 0), axis=1)
    at_a = N * (TALL_B // PAGE) + inverse(piece_a)[:, None] * (TALL_A // PAGE) + pages
    at_b = inverse(piece_b)[:, None] * (TALL_B // PAGE) + pages - PAGES_A
    in_a = pages < PAGES_A
    key_place = jnp.where(in_a, at_a, at_b)
    value_place = key_place + jnp.where(in_a, PAGES_A, PAGES_B)
    finished = (pages < PAGES) & ((pages + 1) * PAGE <= lengths[:, None])
    key_place = jnp.where(finished, key_place, -1)
    value_place = jnp.where(finished, value_place, -1)
    return key_place.reshape(2 * N), value_place.reshape(2 * N)


def live_counts(me, lengths, piece_a, piece_b):
    count_a = jnp.where(piece_a < me, jnp.minimum(pick(lengths, piece_a), ROWS_A), 0)
    count_b = jnp.where(piece_b < me, jnp.maximum(pick(lengths, piece_b) - ROWS_A, 0), 0)
    return count_a, count_b


def body(queries, keys, values, lengths, page_owner):
    me = lax.axis_index("ctx")
    live = jnp.sum(jnp.where(jnp.arange(N, dtype=jnp.int32) == me, lengths, 0)).reshape(1)
    gathered, own, beside, across = exchange(*payloads(keys, values, page_owner))
    piece_a, piece_b = layout(me)
    count_a, count_b = live_counts(me, lengths, piece_a, piece_b)
    key_place, value_place = page_places(me, gathered, piece_a, piece_b, lengths)
    state = early_attention(own, beside, count_b, live, (queries, keys, values))
    outgoing = select_pages(
        (key_place, value_place), own + beside + across + [gathered], state[1]
    )
    decode_cache = lax.all_to_all(
        outgoing.reshape(2 * N, PAGE, 1, 2 * HD), "tp", split_axis=0, concat_axis=2, tiled=True
    )
    attended = late_attention(gathered, across, count_a, count_b, live, state)
    return (attended, decode_cache.reshape((1,) + decode_cache.shape))


def solution(mesh):
    in_specs = (P("ctx", "tp"), P("ctx", "tp"), P("ctx", "tp"), P(), P("ctx", None))
    out_specs = (P("ctx", "tp"), P("ctx", "tp", None, None, None))
    return jax.shard_map(body, mesh=mesh, in_specs=in_specs, out_specs=out_specs, check_vma=False)
```

```python
import math

import jax
import jax.numpy as jnp
from jax import lax
from jax.experimental import pallas as pl
from jax.experimental.pallas import tpu as pltpu
from jax.sharding import PartitionSpec as P

HD = 128
PAGE = 2
NX = 4
NZ = 16
N = NX * NZ
CAP = 192
ROWS_A = 96
ROWS_B = CAP - ROWS_A
PAGES = CAP // PAGE
PAGES_A = ROWS_A // PAGE
PAGES_B = ROWS_B // PAGE
PAD = 16
TALL_A = 2 * ROWS_A + PAD
TALL_B = 2 * ROWS_B
GROUP = 8
ROWS = GROUP * CAP
TILES = 2
TILE = ROWS // TILES
WIDTH = 512
DEAD = -1e30
SCALE = math.log2(math.e) / math.sqrt(HD)
LIMIT = 2.0**64
VMEM_LIMIT = 56 * 1024 * 1024

X_ORDER = [0, -1, 1, 2]
Z_ORDER = [4, 0, -4, 8]
Z_GROUPS = [[x * NZ + z for z in range(NZ)] for x in range(NX)]
STEP = 4
Z_ALL = [d + s for d in (0, -1, 1) for s in Z_ORDER] + [-2, -6, 6, 2]


def shift(value, dx, dz):
    pairs = [
        (x * NZ + z, ((x + dx) % NX) * NZ + (z + dz) % NZ) for x in range(NX) for z in range(NZ)
    ]
    return lax.ppermute(value, "ctx", pairs)


def gather_z(value):
    return lax.all_gather(value, "ctx", axis=0, tiled=False, axis_index_groups=Z_GROUPS)


def exchange(a, b):
    near = [shift(a, dx, 0) for dx in (1, -1, 2)]
    left, right = shift(b, 0, 4), shift(b, 0, -4)
    gathered = gather_z(jnp.stack([a] + near)).reshape(N, TALL_A, HD)
    far = jnp.concatenate([shift(left[:ROWS_B], 0, 4), shift(right[ROWS_B:], 0, -4)], axis=0)
    first = jnp.stack([right, b, left, far])
    own = jnp.concatenate(
        [
            first,
            shift(first, 0, 1),
            shift(first, 0, -1),
            shift(first[1:3], 0, 2),
            shift(first[:2], 0, -2),
        ],
        axis=0,
    )
    left, right = shift(own, 1, 0), shift(own, -1, 0)
    far_left, far_right = shift(left[:8], 1, 0), shift(right[8:], -1, 0)
    return gathered, [own], [left, right], [far_left, far_right]


def lanes(rows):
    return lax.broadcasted_iota(jnp.int32, (rows, HD), 1)


def reference_columns(m):
    rows = m.shape[0]
    m = jnp.broadcast_to(m, (rows, HD))
    high = m.astype(jnp.bfloat16).astype(jnp.float32)
    rest = m - high
    middle = rest.astype(jnp.bfloat16).astype(jnp.float32)
    low = rest - middle
    lane = lanes(rows)
    out = jnp.where(lane == 0, 1.0, 0.0)
    out = jnp.where(lane == 1, -high, out)
    out = jnp.where(lane == 2, -middle, out)
    out = jnp.where(lane == 3, -low, out)
    return out.astype(jnp.bfloat16)


def dot_t(a, b):
    return lax.dot_general(a, b, (((1,), (1,)), ((), ())), preferred_element_type=jnp.float32)


def by_lanes(op, s):
    out = s[:, :HD]
    for i in range(1, s.shape[1] // HD):
        out = op(out, s[:, i * HD : (i + 1) * HD])
    return out


def attention_kernel(first, last, talls, counts, *refs):
    n_src = len(talls)
    count_ref, live_ref = refs[0], refs[1]
    sources = refs[2 : 2 + n_src]
    refs = refs[2 + n_src :]
    if first:
        (q_ref, k_ref, v_ref), refs = refs[:3], refs[3:]
    else:
        (q0, acc0), refs = refs[:2], refs[2:]
    if last:
        out_ref, refs = refs[0], refs[1:]
    q1, acc1, kbuf, vbuf, sems = refs[:5]
    stages, refs = refs[5 : 5 + n_src], refs[5 + n_src :]
    if first:
        q0, acc0 = refs
    live = live_ref[0]

    copies = [
        pltpu.make_async_copy(sources[i], stages[i], sems.at[i]) for i in range(n_src)
    ]
    for copy in copies:
        copy.start()

    if first:
        row = lax.broadcasted_iota(jnp.int32, (CAP, CAP), 0)
        col = lax.broadcasted_iota(jnp.int32, (CAP, CAP), 1)
        bias = jnp.where((col <= row) & (col < live), 0.0, DEAD).astype(jnp.float32)
        for h in range(GROUP):
            at = slice(h * CAP, (h + 1) * CAP)
            q = q_ref[:, h * HD : (h + 1) * HD]
            s = dot_t(q, k_ref[...]) + bias
            top = jnp.max(s, axis=1, keepdims=True)
            p = jnp.exp2((s - top) * SCALE)
            q0[at, 0:HD] = q
            q0[at, HD : 2 * HD] = reference_columns(top)
            acc0[at, 0:HD] = jnp.dot(
                p.astype(jnp.bfloat16), v_ref[...], preferred_element_type=jnp.float32
            )
            acc0[at, HD : 2 * HD] = jnp.where(
                lanes(CAP) == 0, jnp.sum(p, axis=1, keepdims=True), 0.0
            )

    q1[...] = q0[...]
    acc1[...] = acc0[...]

    height = kbuf.shape[0]
    lane = lanes(16)
    alive = jnp.where((lane >= 1) & (lane <= 3), 1.0, 0.0).astype(jnp.float32)
    dead = jnp.where(lane == 0, DEAD, 0.0).astype(jnp.float32)
    step = lax.broadcasted_iota(jnp.int32, (16, HD), 0)
    fill = lanes(WIDTH)
    fill_alive = jnp.where((fill >= 1) & (fill <= 3), 1.0, 0.0).astype(jnp.bfloat16)
    fill_dead = jnp.where(fill == 0, DEAD, 0.0).astype(jnp.bfloat16)
    fill_ones = jnp.where(fill == 0, 1.0, 0.0).astype(jnp.bfloat16)
    for i in range(height // WIDTH):
        at = slice(i * WIDTH, (i + 1) * WIDTH)
        kbuf[at, HD : 2 * HD] = fill_alive
        vbuf[at, HD : 2 * HD] = fill_ones

    for copy in copies:
        copy.wait()

    off = jnp.int32(0)
    base = 0
    for i in range(n_src):

        def pack(j, off, base=base, tall=talls[i], stage=stages[i]):
            count = count_ref[base + j]
            at = pl.ds(pl.multiple_of(off, 16), tall)
            kbuf[at, 0:HD] = stage[j, 0:tall, :]
            vbuf[at, 0:HD] = stage[j, tall : 2 * tall, :]
            whole = (count // 16) * 16
            part = count - whole

            @pl.when(part > 0)
            def _():
                edge = pl.ds(pl.multiple_of(off + whole, 16), 16)
                kbuf[edge, HD : 2 * HD] = jnp.where(step < part, alive, dead).astype(jnp.bfloat16)

            return off + ((count + 15) // 16) * 16

        off = lax.fori_loop(0, counts[i], pack, off)
        base += counts[i]
    at = pl.ds(pl.multiple_of(off, 16), WIDTH)
    kbuf[at, 0:HD] = jnp.zeros((WIDTH, HD), jnp.bfloat16)
    kbuf[at, HD : 2 * HD] = fill_dead
    vbuf[at, 0:HD] = jnp.zeros((WIDTH, HD), jnp.bfloat16)
    blocks = (off + WIDTH - 1) // WIDTH

    def block(i, track):
        at = pl.ds(pl.multiple_of(i * WIDTH, WIDTH), WIDTH)
        for t in range(TILES):
            rows = slice(t * TILE, (t + 1) * TILE)
            p = jnp.exp2(dot_t(q1[rows, :], kbuf[at, :]) * SCALE).astype(jnp.bfloat16)
            track = jnp.maximum(
                track, jnp.max(by_lanes(jnp.maximum, p).reshape(TILE // 16, 16, HD), axis=0)
            )
            acc1[rows, :] += jnp.dot(p, vbuf[at, :], preferred_element_type=jnp.float32)
        return track

    none = jnp.zeros((16, HD), jnp.bfloat16)
    track = lax.fori_loop(0, blocks, block, none)

    @pl.when(jnp.max(track.astype(jnp.float32)) > LIMIT)
    def _():
        for t in range(TILES):
            rows = slice(t * TILE, (t + 1) * TILE)

            def highest(i, top, rows=rows):
                at = pl.ds(pl.multiple_of(i * WIDTH, WIDTH), WIDTH)
                return jnp.maximum(top, by_lanes(jnp.maximum, dot_t(q0[rows, :], kbuf[at, :])))

            top = lax.fori_loop(0, blocks, highest, jnp.zeros((TILE, HD), jnp.float32))
            rise = jnp.max(top, axis=1, keepdims=True)
            columns = q0[rows, HD : 2 * HD].astype(jnp.float32)
            lane = lanes(TILE)
            m = -jnp.sum(
                jnp.where((lane >= 1) & (lane <= 3), columns, 0.0), axis=1, keepdims=True
            )
            q1[rows, HD : 2 * HD] = reference_columns(m + rise)
            acc1[rows, :] = acc0[rows, :] * jnp.exp2(-rise * SCALE)
        lax.fori_loop(0, blocks, block, none)

    if last:
        ok = lax.broadcasted_iota(jnp.int32, (CAP, HD), 0) < live
        for h in range(GROUP):
            at = slice(h * CAP, (h + 1) * CAP)
            total = jnp.sum(acc1[at, HD : 2 * HD], axis=1, keepdims=True)
            result = jnp.where(ok, acc1[at, 0:HD] / total, 0.0)
            out_ref[:, h * HD : (h + 1) * HD] = result.astype(jnp.bfloat16)


def attention(first, last, count, live, sources, state, interpret=False):
    talls = [ROWS_B if s.shape[1] == TALL_B else ROWS_A for s in sources]
    counts = [s.shape[0] for s in sources]
    keys = sum(c * t for c, t in zip(counts, talls))
    height = (keys // WIDTH + 2) * WIDTH
    vmem = pl.BlockSpec(memory_space=pltpu.VMEM)
    smem = pl.BlockSpec(memory_space=pltpu.SMEM)
    state_shapes = [
        ((ROWS, 2 * HD), jnp.bfloat16),
        ((ROWS, 2 * HD), jnp.float32),
    ]
    scratch_state = [pltpu.VMEM(*s) for s in state_shapes]
    if last:
        out_shape = jax.ShapeDtypeStruct((CAP, GROUP * HD), jnp.bfloat16)
        out_specs = vmem
    else:
        out_shape = [jax.ShapeDtypeStruct(*s) for s in state_shapes]
        out_specs = [vmem] * 2
    scratch = (
        (scratch_state if last else [])
        + [
            pltpu.VMEM((height, 2 * HD), jnp.bfloat16),
            pltpu.VMEM((height, 2 * HD), jnp.bfloat16),
            pltpu.SemaphoreType.DMA((len(sources),)),
        ]
        + [pltpu.VMEM(s.shape, jnp.bfloat16) for s in sources]
        + (scratch_state if first else [])
    )

    def kernel(*refs):
        attention_kernel(first, last, talls, counts, *refs)

    return pl.pallas_call(
        kernel,
        out_shape=out_shape,
        in_specs=[smem, smem] + [pl.BlockSpec(memory_space=pl.ANY)] * len(sources)
        + [vmem] * len(state),
        out_specs=out_specs,
        scratch_shapes=scratch,
        compiler_params=pltpu.CompilerParams(vmem_limit_bytes=VMEM_LIMIT),
        cost_estimate=pl.CostEstimate(
            flops=8 * ROWS * keys * HD, bytes_accessed=8 << 20, transcendentals=0
        ),
        interpret=interpret,
    )(count, live, *sources, *state)


def early_attention(own, beside, count_b, live, arrays, interpret=False):
    state = attention(True, False, count_b[:16], live, own, arrays, interpret)
    return attention(False, False, count_b[16:48], live, beside, state, interpret)


def late_attention(gathered, across, count_a, count_b, live, state, interpret=False):
    count = jnp.concatenate([count_b[48:], count_a])
    return attention(False, True, count, live, across + [gathered], state, interpret)


def select_kernel(n_src, key_ref, value_ref, after_ref, *refs):
    sources, (out_ref, pages, sems) = refs[:n_src], refs[n_src:]
    copies = []
    start = 0
    for i, source in enumerate(sources):
        count = source.shape[0]
        copies.append(
            pltpu.make_async_copy(source, pages.at[pl.ds(start, count)], sems.at[i])
        )
        start += count
    for copy in copies:
        copy.start()
    for copy in copies:
        copy.wait()

    def one(s, carry):
        place = key_ref[s]
        keep = jnp.where(place >= 0, 1.0, 0.0).astype(jnp.bfloat16)
        out_ref[s, :, 0:HD] = pages[jnp.maximum(place, 0)] * keep
        out_ref[s, :, HD : 2 * HD] = pages[jnp.maximum(value_ref[s], 0)] * keep
        return carry

    lax.fori_loop(0, 2 * N, one, 0, unroll=4)


def select_pages(places, sources, after, interpret=False):
    sources = [s.reshape(s.shape[0] * s.shape[1] // PAGE, PAGE, HD) for s in sources]
    total = sum(s.shape[0] for s in sources)
    smem = pl.BlockSpec(memory_space=pltpu.SMEM)
    anywhere = pl.BlockSpec(memory_space=pl.ANY)

    def kernel(*refs):
        select_kernel(len(sources), *refs)

    return pl.pallas_call(
        kernel,
        out_shape=jax.ShapeDtypeStruct((2 * N, PAGE, 2 * HD), jnp.bfloat16),
        in_specs=[smem] * 2 + [anywhere] * (1 + len(sources)),
        out_specs=pl.BlockSpec(memory_space=pltpu.VMEM),
        scratch_shapes=[
            pltpu.VMEM((total, PAGE, HD), jnp.bfloat16),
            pltpu.SemaphoreType.DMA((len(sources),)),
        ],
        compiler_params=pltpu.CompilerParams(vmem_limit_bytes=VMEM_LIMIT),
        cost_estimate=pl.CostEstimate(flops=0, bytes_accessed=8 << 20, transcendentals=0),
        interpret=interpret,
    )(*places, after, *sources)


def payload_kernel(k_ref, v_ref, owner_ref, a_ref, b_ref):
    a_ref[0:ROWS_A, :] = k_ref[0:ROWS_A, :]
    a_ref[ROWS_A : 2 * ROWS_A, :] = v_ref[0:ROWS_A, :]
    a_ref[2 * ROWS_A :, :] = jnp.zeros((PAD, HD), jnp.bfloat16)
    owner = jnp.broadcast_to(owner_ref[...].astype(jnp.float32), (PAD, PAGES))
    a_ref[2 * ROWS_A :, 0:PAGES] = owner.astype(jnp.bfloat16)
    b_ref[0:ROWS_B, :] = k_ref[ROWS_A:, :]
    b_ref[ROWS_B:, :] = v_ref[ROWS_A:, :]


def payloads(keys, values, page_owner, interpret=False):
    vmem = pl.BlockSpec(memory_space=pltpu.VMEM)
    return pl.pallas_call(
        payload_kernel,
        out_shape=[
            jax.ShapeDtypeStruct((TALL_A, HD), jnp.bfloat16),
            jax.ShapeDtypeStruct((TALL_B, HD), jnp.bfloat16),
        ],
        in_specs=[vmem] * 3,
        out_specs=[vmem] * 2,
        interpret=interpret,
    )(keys, values, page_owner.reshape(1, PAGES))


def layout(me):
    mx, mz = me // NZ, me % NZ
    dx = jnp.array([0] * 16 + [-1] * 16 + [1] * 16 + [2] * 16, jnp.int32)
    dz = jnp.array(Z_ALL * NX, jnp.int32)
    piece_b = ((mx + dx + NX) % NX) * NZ + (mz + dz + NZ) % NZ
    dx = jnp.array(X_ORDER * NZ, jnp.int32)
    piece_a = ((mx + dx + NX) % NX) * NZ + jnp.arange(N, dtype=jnp.int32) // NX
    return piece_a, piece_b


def pick(table, index):
    place = jnp.arange(N, dtype=jnp.int32)
    return jnp.sum(jnp.where(index[:, None] == place[None, :], table[None, :], 0), axis=1)


def inverse(index):
    place = jnp.arange(N, dtype=jnp.int32)
    return jnp.sum(jnp.where(index[None, :] == place[:, None], place[None, :], 0), axis=1)


def page_places(me, gathered, piece_a, piece_b, lengths):
    place = jnp.arange(N, dtype=jnp.int32)
    owners = gathered[:, 2 * ROWS_A, :PAGES]
    page = jnp.arange(PAGES, dtype=jnp.int32)[None, :]
    match = owners == me.astype(jnp.bfloat16)
    low = jnp.min(jnp.where(match, page, PAGES), axis=1)
    high = jnp.max(jnp.where(match, page, -1), axis=1)
    pages = jnp.stack([low, jnp.where(high > low, high, PAGES)], axis=1)
    hit = piece_a[None, :] == place[:, None]
    pages = jnp.sum(jnp.where(hit[:, :, None], pages[None, :, :], 0), axis=1)
    at_a = N * (TALL_B // PAGE) + inverse(piece_a)[:, None] * (TALL_A // PAGE) + pages
    at_b = inverse(piece_b)[:, None] * (TALL_B // PAGE) + pages - PAGES_A
    in_a = pages < PAGES_A
    key_place = jnp.where(in_a, at_a, at_b)
    value_place = key_place + jnp.where(in_a, PAGES_A, PAGES_B)
    finished = (pages < PAGES) & ((pages + 1) * PAGE <= lengths[:, None])
    key_place = jnp.where(finished, key_place, -1)
    value_place = jnp.where(finished, value_place, -1)
    return key_place.reshape(2 * N), value_place.reshape(2 * N)


def live_counts(me, lengths, piece_a, piece_b):
    count_a = jnp.where(piece_a < me, jnp.minimum(pick(lengths, piece_a), ROWS_A), 0)
    count_b = jnp.where(piece_b < me, jnp.maximum(pick(lengths, piece_b) - ROWS_A, 0), 0)
    return count_a, count_b


def body(queries, keys, values, lengths, page_owner):
    me = lax.axis_index("ctx")
    live = jnp.sum(jnp.where(jnp.arange(N, dtype=jnp.int32) == me, lengths, 0)).reshape(1)
    gathered, own, beside, across = exchange(*payloads(keys, values, page_owner))
    piece_a, piece_b = layout(me)
    own, lengths = lax.optimization_barrier((own, lengths))
    count_a, count_b = live_counts(me, lengths, piece_a, piece_b)
    key_place, value_place = page_places(me, gathered, piece_a, piece_b, lengths)
    state = early_attention(own, beside, count_b, live, (queries, keys, values))
    outgoing = select_pages(
        (key_place, value_place), own + beside + across + [gathered], state[1]
    )
    decode_cache = lax.all_to_all(
        outgoing.reshape(2 * N, PAGE, 1, 2 * HD), "tp", split_axis=0, concat_axis=2, tiled=True
    )
    attended = late_attention(gathered, across, count_a, count_b, live, state)
    return (attended, decode_cache.reshape((1,) + decode_cache.shape))


def solution(mesh):
    in_specs = (P("ctx", "tp"), P("ctx", "tp"), P("ctx", "tp"), P(), P("ctx", None))
    out_specs = (P("ctx", "tp"), P("ctx", "tp", None, None, None))
    return jax.shard_map(body, mesh=mesh, in_specs=in_specs, out_specs=out_specs, check_vma=False)
```

```python
import math

import jax
import jax.numpy as jnp
from jax import lax
from jax.experimental import pallas as pl
from jax.experimental.pallas import tpu as pltpu
from jax.sharding import PartitionSpec as P

HD = 128
PAGE = 2
NX = 4
NZ = 16
N = NX * NZ
CAP = 192
ROWS_A = 96
ROWS_B = CAP - ROWS_A
PAGES = CAP // PAGE
PAGES_A = ROWS_A // PAGE
PAGES_B = ROWS_B // PAGE
PAD = 16
TALL_A = 2 * ROWS_A + PAD
TALL_B = 2 * ROWS_B
GROUP = 8
ROWS = GROUP * CAP
TILES = 2
TILE = ROWS // TILES
WIDTH = 512
DEAD = -1e30
SCALE = math.log2(math.e) / math.sqrt(HD)
LIMIT = 2.0**64
VMEM_LIMIT = 56 * 1024 * 1024

X_ORDER = [0, -1, 1, 2]
Z_ORDER = [4, 0, -4, 8]
Z_GROUPS = [[x * NZ + z for z in range(NZ)] for x in range(NX)]
STEP = 4
Z_ALL = [d + s for d in (0, -1, 1) for s in Z_ORDER] + [-2, -6, 6, 2]


def shift(value, dx, dz):
    pairs = [
        (x * NZ + z, ((x + dx) % NX) * NZ + (z + dz) % NZ) for x in range(NX) for z in range(NZ)
    ]
    return lax.ppermute(value, "ctx", pairs)


def gather_z(value):
    return lax.all_gather(value, "ctx", axis=0, tiled=False, axis_index_groups=Z_GROUPS)


def exchange(a, b):
    near = [shift(a, dx, 0) for dx in (1, -1, 2)]
    left, right = shift(b, 0, 4), shift(b, 0, -4)
    gathered = gather_z(jnp.stack([a] + near)).reshape(N, TALL_A, HD)
    far = jnp.concatenate([shift(left[:ROWS_B], 0, 4), shift(right[ROWS_B:], 0, -4)], axis=0)
    first = jnp.stack([right, b, left, far])
    own = jnp.concatenate(
        [
            first,
            shift(first, 0, 1),
            shift(first, 0, -1),
            shift(first[1:3], 0, 2),
            shift(first[:2], 0, -2),
        ],
        axis=0,
    )
    left, right = shift(own, 1, 0), shift(own, -1, 0)
    far_left, far_right = shift(left[:8], 1, 0), shift(right[8:], -1, 0)
    return gathered, [own], [left, right], [far_left, far_right]


def lanes(rows):
    return lax.broadcasted_iota(jnp.int32, (rows, HD), 1)


def dot_t(a, b):
    return lax.dot_general(a, b, (((1,), (1,)), ((), ())), preferred_element_type=jnp.float32)


def by_lanes(op, s):
    out = s[:, :HD]
    for i in range(1, s.shape[1] // HD):
        out = op(out, s[:, i * HD : (i + 1) * HD])
    return out


def attention_kernel(first, last, talls, counts, *refs):
    n_src = len(talls)
    count_ref, live_ref = refs[0], refs[1]
    sources = refs[2 : 2 + n_src]
    refs = refs[2 + n_src :]
    if first:
        (q_ref, k_ref, v_ref), refs = refs[:3], refs[3:]
    else:
        (q_ref, m0, acc0), refs = refs[:3], refs[3:]
    if last:
        out_ref, refs = refs[0], refs[1:]
    m1, acc1, qs, kbuf, vbuf, sems = refs[:6]
    stages, refs = refs[6 : 6 + n_src], refs[6 + n_src :]
    if first:
        m0, acc0 = refs
    live = live_ref[0]

    copies = [
        pltpu.make_async_copy(sources[i], stages[i], sems.at[i]) for i in range(n_src)
    ]
    for copy in copies:
        copy.start()

    for h in range(GROUP):
        qs[h * CAP : (h + 1) * CAP, :] = q_ref[:, h * HD : (h + 1) * HD]

    if first:
        row = lax.broadcasted_iota(jnp.int32, (CAP, CAP), 0)
        col = lax.broadcasted_iota(jnp.int32, (CAP, CAP), 1)
        bias = jnp.where((col <= row) & (col < live), 0.0, DEAD).astype(jnp.float32)
        for h in range(GROUP):
            at = slice(h * CAP, (h + 1) * CAP)
            s = dot_t(qs[at, :], k_ref[...]) * SCALE + bias
            top = jnp.max(s, axis=1, keepdims=True)
            p = jnp.exp2(s - top)
            m0[at, :] = jnp.broadcast_to(top, (CAP, HD))
            acc0[at, 0:HD] = jnp.dot(
                p.astype(jnp.bfloat16), v_ref[...], preferred_element_type=jnp.float32
            )
            acc0[at, HD : 2 * HD] = jnp.where(
                lanes(CAP) == 0, jnp.sum(p, axis=1, keepdims=True), 0.0
            )

    m1[...] = m0[...]
    acc1[...] = acc0[...]

    height = kbuf.shape[0]
    step = lax.broadcasted_iota(jnp.int32, (16, HD), 0)
    lead = jnp.where(lanes(16) == 0, 1.0, 0.0).astype(jnp.float32)
    ones = jnp.where(lanes(WIDTH) == 0, 1.0, 0.0).astype(jnp.bfloat16)
    for i in range(height // WIDTH):
        vbuf[i * WIDTH : (i + 1) * WIDTH, HD : 2 * HD] = ones

    for copy in copies:
        copy.wait()

    off = jnp.int32(0)
    base = 0
    for i in range(n_src):

        def pack(j, off, base=base, tall=talls[i], stage=stages[i]):
            count = count_ref[base + j]
            at = pl.ds(pl.multiple_of(off, 16), tall)
            kbuf[at, :] = stage[j, 0:tall, :]
            vbuf[at, 0:HD] = stage[j, tall : 2 * tall, :]
            whole = (count // 16) * 16
            part = count - whole

            @pl.when(part > 0)
            def _():
                edge = pl.ds(pl.multiple_of(off + whole, 16), 16)
                keep = step < part
                k = kbuf[edge, :].astype(jnp.float32)
                k = jnp.where(keep, k, jnp.broadcast_to(k[0:1, :], (16, HD)))
                kbuf[edge, :] = k.astype(jnp.bfloat16)
                v = jnp.where(keep, vbuf[edge, 0:HD].astype(jnp.float32), 0.0)
                vbuf[edge, 0:HD] = v.astype(jnp.bfloat16)
                vbuf[edge, HD : 2 * HD] = jnp.where(keep, lead, 0.0).astype(jnp.bfloat16)

            return off + ((count + 15) // 16) * 16

        off = lax.fori_loop(0, counts[i], pack, off)
        base += counts[i]
    at = pl.ds(pl.multiple_of(off, 16), WIDTH)
    k = kbuf[0:16, :].astype(jnp.float32)
    kbuf[at, :] = jnp.broadcast_to(k[0:1, :], (WIDTH, HD)).astype(jnp.bfloat16)
    vbuf[at, :] = jnp.zeros((WIDTH, 2 * HD), jnp.bfloat16)
    blocks = (off + WIDTH - 1) // WIDTH

    def block(i, track):
        at = pl.ds(pl.multiple_of(i * WIDTH, WIDTH), WIDTH)
        for t in range(TILES):
            rows = slice(t * TILE, (t + 1) * TILE)
            m = jnp.concatenate([m1[rows, :]] * (WIDTH // HD), axis=1)
            p = jnp.exp2(dot_t(qs[rows, :], kbuf[at, :]) * SCALE - m).astype(jnp.bfloat16)
            track = jnp.maximum(
                track, jnp.max(by_lanes(jnp.maximum, p).reshape(TILE // 16, 16, HD), axis=0)
            )
            acc1[rows, :] += jnp.dot(p, vbuf[at, :], preferred_element_type=jnp.float32)
        return track

    none = jnp.zeros((16, HD), jnp.bfloat16)
    track = lax.fori_loop(0, blocks, block, none)

    @pl.when(jnp.max(track.astype(jnp.float32)) > LIMIT)
    def _():
        for t in range(TILES):
            rows = slice(t * TILE, (t + 1) * TILE)

            def highest(i, top, rows=rows):
                at = pl.ds(pl.multiple_of(i * WIDTH, WIDTH), WIDTH)
                return jnp.maximum(top, by_lanes(jnp.maximum, dot_t(qs[rows, :], kbuf[at, :])))

            top = lax.fori_loop(0, blocks, highest, jnp.full((TILE, HD), DEAD, jnp.float32))
            old = m0[rows, :]
            m = jnp.maximum(old, jnp.max(top, axis=1, keepdims=True) * SCALE)
            factor = jnp.exp2(old - m)
            m1[rows, :] = m
            acc1[rows, :] = acc0[rows, :] * jnp.concatenate([factor, factor], axis=1)
        lax.fori_loop(0, blocks, block, none)

    if last:
        ok = lax.broadcasted_iota(jnp.int32, (CAP, HD), 0) < live
        for h in range(GROUP):
            at = slice(h * CAP, (h + 1) * CAP)
            total = jnp.sum(acc1[at, HD : 2 * HD], axis=1, keepdims=True)
            result = jnp.where(ok, acc1[at, 0:HD] / total, 0.0)
            out_ref[:, h * HD : (h + 1) * HD] = result.astype(jnp.bfloat16)


def attention(first, last, count, live, sources, state, interpret=False):
    talls = [ROWS_B if s.shape[1] == TALL_B else ROWS_A for s in sources]
    counts = [s.shape[0] for s in sources]
    keys = sum(c * t for c, t in zip(counts, talls))
    height = (keys // WIDTH + 2) * WIDTH
    vmem = pl.BlockSpec(memory_space=pltpu.VMEM)
    smem = pl.BlockSpec(memory_space=pltpu.SMEM)
    state_shapes = [
        ((ROWS, HD), jnp.float32),
        ((ROWS, 2 * HD), jnp.float32),
    ]
    scratch_state = [pltpu.VMEM(*s) for s in state_shapes]
    if last:
        out_shape = jax.ShapeDtypeStruct((CAP, GROUP * HD), jnp.bfloat16)
        out_specs = vmem
    else:
        out_shape = [jax.ShapeDtypeStruct(*s) for s in state_shapes]
        out_specs = [vmem] * 2
    scratch = (
        (scratch_state if last else [])
        + [
            pltpu.VMEM((ROWS, HD), jnp.bfloat16),
            pltpu.VMEM((height, HD), jnp.bfloat16),
            pltpu.VMEM((height, 2 * HD), jnp.bfloat16),
            pltpu.SemaphoreType.DMA((len(sources),)),
        ]
        + [pltpu.VMEM(s.shape, jnp.bfloat16) for s in sources]
        + (scratch_state if first else [])
    )

    def kernel(*refs):
        attention_kernel(first, last, talls, counts, *refs)

    return pl.pallas_call(
        kernel,
        out_shape=out_shape,
        in_specs=[smem, smem] + [pl.BlockSpec(memory_space=pl.ANY)] * len(sources)
        + [vmem] * len(state),
        out_specs=out_specs,
        scratch_shapes=scratch,
        compiler_params=pltpu.CompilerParams(vmem_limit_bytes=VMEM_LIMIT),
        cost_estimate=pl.CostEstimate(
            flops=8 * ROWS * keys * HD, bytes_accessed=8 << 20, transcendentals=0
        ),
        interpret=interpret,
    )(count, live, *sources, *state)


def early_attention(own, beside, count_b, live, arrays, interpret=False):
    state = attention(True, False, count_b[:16], live, own, arrays, interpret)
    state = (arrays[0], *state)
    state = attention(False, False, count_b[16:48], live, beside, state, interpret)
    return (arrays[0], *state)


def late_attention(gathered, across, count_a, count_b, live, state, interpret=False):
    count = jnp.concatenate([count_b[48:], count_a])
    return attention(False, True, count, live, across + [gathered], state, interpret)


def select_kernel(n_src, key_ref, value_ref, after_ref, *refs):
    sources, (out_ref, pages, sems) = refs[:n_src], refs[n_src:]
    copies = []
    start = 0
    for i, source in enumerate(sources):
        count = source.shape[0]
        copies.append(
            pltpu.make_async_copy(source, pages.at[pl.ds(start, count)], sems.at[i])
        )
        start += count
    for copy in copies:
        copy.start()
    for copy in copies:
        copy.wait()

    def one(s, carry):
        place = key_ref[s]
        keep = jnp.where(place >= 0, 1.0, 0.0).astype(jnp.bfloat16)
        out_ref[s, :, 0:HD] = pages[jnp.maximum(place, 0)] * keep
        out_ref[s, :, HD : 2 * HD] = pages[jnp.maximum(value_ref[s], 0)] * keep
        return carry

    lax.fori_loop(0, 2 * N, one, 0, unroll=4)


def select_pages(places, sources, after, interpret=False):
    sources = [s.reshape(s.shape[0] * s.shape[1] // PAGE, PAGE, HD) for s in sources]
    total = sum(s.shape[0] for s in sources)
    smem = pl.BlockSpec(memory_space=pltpu.SMEM)
    anywhere = pl.BlockSpec(memory_space=pl.ANY)

    def kernel(*refs):
        select_kernel(len(sources), *refs)

    return pl.pallas_call(
        kernel,
        out_shape=jax.ShapeDtypeStruct((2 * N, PAGE, 2 * HD), jnp.bfloat16),
        in_specs=[smem] * 2 + [anywhere] * (1 + len(sources)),
        out_specs=pl.BlockSpec(memory_space=pltpu.VMEM),
        scratch_shapes=[
            pltpu.VMEM((total, PAGE, HD), jnp.bfloat16),
            pltpu.SemaphoreType.DMA((len(sources),)),
        ],
        compiler_params=pltpu.CompilerParams(vmem_limit_bytes=VMEM_LIMIT),
        cost_estimate=pl.CostEstimate(flops=0, bytes_accessed=8 << 20, transcendentals=0),
        interpret=interpret,
    )(*places, after, *sources)


def payload_kernel(k_ref, v_ref, owner_ref, a_ref, b_ref):
    a_ref[0:ROWS_A, :] = k_ref[0:ROWS_A, :]
    a_ref[ROWS_A : 2 * ROWS_A, :] = v_ref[0:ROWS_A, :]
    a_ref[2 * ROWS_A :, :] = jnp.zeros((PAD, HD), jnp.bfloat16)
    owner = jnp.broadcast_to(owner_ref[...].astype(jnp.float32), (PAD, PAGES))
    a_ref[2 * ROWS_A :, 0:PAGES] = owner.astype(jnp.bfloat16)
    b_ref[0:ROWS_B, :] = k_ref[ROWS_A:, :]
    b_ref[ROWS_B:, :] = v_ref[ROWS_A:, :]


def payloads(keys, values, page_owner, interpret=False):
    vmem = pl.BlockSpec(memory_space=pltpu.VMEM)
    return pl.pallas_call(
        payload_kernel,
        out_shape=[
            jax.ShapeDtypeStruct((TALL_A, HD), jnp.bfloat16),
            jax.ShapeDtypeStruct((TALL_B, HD), jnp.bfloat16),
        ],
        in_specs=[vmem] * 3,
        out_specs=[vmem] * 2,
        interpret=interpret,
    )(keys, values, page_owner.reshape(1, PAGES))


def layout(me):
    mx, mz = me // NZ, me % NZ
    dx = jnp.array([0] * 16 + [-1] * 16 + [1] * 16 + [2] * 16, jnp.int32)
    dz = jnp.array(Z_ALL * NX, jnp.int32)
    piece_b = ((mx + dx + NX) % NX) * NZ + (mz + dz + NZ) % NZ
    dx = jnp.array(X_ORDER * NZ, jnp.int32)
    piece_a = ((mx + dx + NX) % NX) * NZ + jnp.arange(N, dtype=jnp.int32) // NX
    return piece_a, piece_b


def pick(table, index):
    place = jnp.arange(N, dtype=jnp.int32)
    return jnp.sum(jnp.where(index[:, None] == place[None, :], table[None, :], 0), axis=1)


def inverse(index):
    place = jnp.arange(N, dtype=jnp.int32)
    return jnp.sum(jnp.where(index[None, :] == place[:, None], place[None, :], 0), axis=1)


def page_places(me, gathered, piece_a, piece_b, lengths):
    place = jnp.arange(N, dtype=jnp.int32)
    owners = gathered[:, 2 * ROWS_A, :PAGES]
    page = jnp.arange(PAGES, dtype=jnp.int32)[None, :]
    match = owners == me.astype(jnp.bfloat16)
    low = jnp.min(jnp.where(match, page, PAGES), axis=1)
    high = jnp.max(jnp.where(match, page, -1), axis=1)
    pages = jnp.stack([low, jnp.where(high > low, high, PAGES)], axis=1)
    hit = piece_a[None, :] == place[:, None]
    pages = jnp.sum(jnp.where(hit[:, :, None], pages[None, :, :], 0), axis=1)
    at_a = N * (TALL_B // PAGE) + inverse(piece_a)[:, None] * (TALL_A // PAGE) + pages
    at_b = inverse(piece_b)[:, None] * (TALL_B // PAGE) + pages - PAGES_A
    in_a = pages < PAGES_A
    key_place = jnp.where(in_a, at_a, at_b)
    value_place = key_place + jnp.where(in_a, PAGES_A, PAGES_B)
    finished = (pages < PAGES) & ((pages + 1) * PAGE <= lengths[:, None])
    key_place = jnp.where(finished, key_place, -1)
    value_place = jnp.where(finished, value_place, -1)
    return key_place.reshape(2 * N), value_place.reshape(2 * N)


def live_counts(me, lengths, piece_a, piece_b):
    count_a = jnp.where(piece_a < me, jnp.minimum(pick(lengths, piece_a), ROWS_A), 0)
    count_b = jnp.where(piece_b < me, jnp.maximum(pick(lengths, piece_b) - ROWS_A, 0), 0)
    return count_a, count_b


def body(queries, keys, values, lengths, page_owner):
    me = lax.axis_index("ctx")
    live = jnp.sum(jnp.where(jnp.arange(N, dtype=jnp.int32) == me, lengths, 0)).reshape(1)
    gathered, own, beside, across = exchange(*payloads(keys, values, page_owner))
    piece_a, piece_b = layout(me)
    own, lengths = lax.optimization_barrier((own, lengths))
    count_a, count_b = live_counts(me, lengths, piece_a, piece_b)
    key_place, value_place = page_places(me, gathered, piece_a, piece_b, lengths)
    state = early_attention(own, beside, count_b, live, (queries, keys, values))
    outgoing = select_pages(
        (key_place, value_place), own + beside + across + [gathered], state[1]
    )
    decode_cache = lax.all_to_all(
        outgoing.reshape(2 * N, PAGE, 1, 2 * HD), "tp", split_axis=0, concat_axis=2, tiled=True
    )
    attended = late_attention(gathered, across, count_a, count_b, live, state)
    return (attended, decode_cache.reshape((1,) + decode_cache.shape))


def solution(mesh):
    in_specs = (P("ctx", "tp"), P("ctx", "tp"), P("ctx", "tp"), P(), P("ctx", None))
    out_specs = (P("ctx", "tp"), P("ctx", "tp", None, None, None))
    return jax.shard_map(body, mesh=mesh, in_specs=in_specs, out_specs=out_specs, check_vma=False)
```

```python
import math

import jax
import jax.numpy as jnp
from jax import lax
from jax.experimental import pallas as pl
from jax.experimental.pallas import tpu as pltpu
from jax.sharding import PartitionSpec as P

HD = 128
PAGE = 2
NX = 4
NZ = 16
N = NX * NZ
CAP = 192
ROWS_A = 96
ROWS_B = CAP - ROWS_A
PAGES = CAP // PAGE
PAGES_A = ROWS_A // PAGE
PAGES_B = ROWS_B // PAGE
PAD = 16
TALL_A = 2 * ROWS_A + PAD
TALL_B = 2 * ROWS_B
GROUP = 8
ROWS = GROUP * CAP
TILES = 4
TILE = ROWS // TILES
WIDTH = 512
DEAD = -1e30
SCALE = math.log2(math.e) / math.sqrt(HD)
LIMIT = 2.0**64
VMEM_LIMIT = 56 * 1024 * 1024

X_ORDER = [0, -1, 1, 2]
Z_ORDER = [4, 0, -4, 8]
Z_GROUPS = [[x * NZ + z for z in range(NZ)] for x in range(NX)]
STEP = 4
Z_ALL = [d + s for d in (0, -1, 1) for s in Z_ORDER] + [-2, -6, 6, 2]


def shift(value, dx, dz):
    pairs = [
        (x * NZ + z, ((x + dx) % NX) * NZ + (z + dz) % NZ) for x in range(NX) for z in range(NZ)
    ]
    return lax.ppermute(value, "ctx", pairs)


def gather_z(value):
    return lax.all_gather(value, "ctx", axis=0, tiled=False, axis_index_groups=Z_GROUPS)


def exchange(a, b):
    near = [shift(a, dx, 0) for dx in (1, -1, 2)]
    left, right = shift(b, 0, 4), shift(b, 0, -4)
    gathered = gather_z(jnp.stack([a] + near)).reshape(N, TALL_A, HD)
    far = jnp.concatenate([shift(left[:ROWS_B], 0, 4), shift(right[ROWS_B:], 0, -4)], axis=0)
    first = jnp.stack([right, b, left, far])
    own = jnp.concatenate(
        [
            first,
            shift(first, 0, 1),
            shift(first, 0, -1),
            shift(first[1:3], 0, 2),
            shift(first[:2], 0, -2),
        ],
        axis=0,
    )
    left, right = shift(own, 1, 0), shift(own, -1, 0)
    far_left, far_right = shift(left[:8], 1, 0), shift(right[8:], -1, 0)
    return gathered, [own], [left, right], [far_left, far_right]


def lanes(rows):
    return lax.broadcasted_iota(jnp.int32, (rows, HD), 1)


def dot_t(a, b):
    return lax.dot_general(a, b, (((1,), (1,)), ((), ())), preferred_element_type=jnp.float32)


def by_lanes(op, s):
    out = s[:, :HD]
    for i in range(1, s.shape[1] // HD):
        out = op(out, s[:, i * HD : (i + 1) * HD])
    return out


def attention_kernel(first, last, talls, counts, *refs):
    n_src = len(talls)
    count_ref, live_ref = refs[0], refs[1]
    sources = refs[2 : 2 + n_src]
    refs = refs[2 + n_src :]
    if first:
        (q_ref, k_ref, v_ref), refs = refs[:3], refs[3:]
    else:
        (q_ref, m0, acc0), refs = refs[:3], refs[3:]
    if last:
        out_ref, refs = refs[0], refs[1:]
    m1, acc1, qs, kbuf, vbuf, sems = refs[:6]
    stages, refs = refs[6 : 6 + n_src], refs[6 + n_src :]
    if first:
        m0, acc0 = refs
    live = live_ref[0]

    copies = [
        pltpu.make_async_copy(sources[i], stages[i], sems.at[i]) for i in range(n_src)
    ]
    for copy in copies:
        copy.start()

    for h in range(GROUP):
        qs[h * CAP : (h + 1) * CAP, :] = q_ref[:, h * HD : (h + 1) * HD]

    if first:
        row = lax.broadcasted_iota(jnp.int32, (CAP, CAP), 0)
        col = lax.broadcasted_iota(jnp.int32, (CAP, CAP), 1)
        bias = jnp.where((col <= row) & (col < live), 0.0, DEAD).astype(jnp.float32)
        for h in range(GROUP):
            at = slice(h * CAP, (h + 1) * CAP)
            s = dot_t(qs[at, :], k_ref[...]) * SCALE + bias
            top = jnp.max(s, axis=1, keepdims=True)
            p = jnp.exp2(s - top)
            m0[at, :] = jnp.broadcast_to(top, (CAP, HD))
            acc0[at, 0:HD] = jnp.dot(
                p.astype(jnp.bfloat16), v_ref[...], preferred_element_type=jnp.float32
            )
            acc0[at, HD : 2 * HD] = jnp.where(
                lanes(CAP) == 0, jnp.sum(p, axis=1, keepdims=True), 0.0
            )

    m1[...] = m0[...]
    acc1[...] = acc0[...]

    height = kbuf.shape[0]
    step = lax.broadcasted_iota(jnp.int32, (16, HD), 0)
    lead = jnp.where(lanes(16) == 0, 1.0, 0.0).astype(jnp.float32)
    ones = jnp.where(lanes(WIDTH) == 0, 1.0, 0.0).astype(jnp.bfloat16)
    for i in range(height // WIDTH):
        vbuf[i * WIDTH : (i + 1) * WIDTH, HD : 2 * HD] = ones

    for copy in copies:
        copy.wait()

    off = jnp.int32(0)
    base = 0
    for i in range(n_src):

        def pack(j, off, base=base, tall=talls[i], stage=stages[i]):
            count = count_ref[base + j]
            at = pl.ds(pl.multiple_of(off, 16), tall)
            kbuf[at, :] = stage[j, 0:tall, :]
            vbuf[at, 0:HD] = stage[j, tall : 2 * tall, :]
            whole = (count // 16) * 16
            part = count - whole

            @pl.when(part > 0)
            def _():
                edge = pl.ds(pl.multiple_of(off + whole, 16), 16)
                keep = step < part
                k = kbuf[edge, :].astype(jnp.float32)
                k = jnp.where(keep, k, jnp.broadcast_to(k[0:1, :], (16, HD)))
                kbuf[edge, :] = k.astype(jnp.bfloat16)
                v = jnp.where(keep, vbuf[edge, 0:HD].astype(jnp.float32), 0.0)
                vbuf[edge, 0:HD] = v.astype(jnp.bfloat16)
                vbuf[edge, HD : 2 * HD] = jnp.where(keep, lead, 0.0).astype(jnp.bfloat16)

            return off + ((count + 15) // 16) * 16

        off = lax.fori_loop(0, counts[i], pack, off)
        base += counts[i]
    at = pl.ds(pl.multiple_of(off, 16), WIDTH)
    k = kbuf[0:16, :].astype(jnp.float32)
    kbuf[at, :] = jnp.broadcast_to(k[0:1, :], (WIDTH, HD)).astype(jnp.bfloat16)
    vbuf[at, :] = jnp.zeros((WIDTH, 2 * HD), jnp.bfloat16)
    blocks = (off + WIDTH - 1) // WIDTH

    def block(i, track):
        at = pl.ds(pl.multiple_of(i * WIDTH, WIDTH), WIDTH)
        scores = dot_t(qs[0:TILE, :], kbuf[at, :])
        for t in range(TILES):
            rows = slice(t * TILE, (t + 1) * TILE)
            ahead = scores
            if t + 1 < TILES:
                ahead = dot_t(qs[(t + 1) * TILE : (t + 2) * TILE, :], kbuf[at, :])
            m = jnp.concatenate([m1[rows, :]] * (WIDTH // HD), axis=1)
            p = jnp.exp2(scores * SCALE - m).astype(jnp.bfloat16)
            track = jnp.maximum(
                track, jnp.max(by_lanes(jnp.maximum, p).reshape(TILE // 16, 16, HD), axis=0)
            )
            acc1[rows, :] += jnp.dot(p, vbuf[at, :], preferred_element_type=jnp.float32)
            scores = ahead
        return track

    none = jnp.zeros((16, HD), jnp.bfloat16)
    track = lax.fori_loop(0, blocks, block, none)

    @pl.when(jnp.max(track.astype(jnp.float32)) > LIMIT)
    def _():
        for t in range(TILES):
            rows = slice(t * TILE, (t + 1) * TILE)

            def highest(i, top, rows=rows):
                at = pl.ds(pl.multiple_of(i * WIDTH, WIDTH), WIDTH)
                return jnp.maximum(top, by_lanes(jnp.maximum, dot_t(qs[rows, :], kbuf[at, :])))

            top = lax.fori_loop(0, blocks, highest, jnp.full((TILE, HD), DEAD, jnp.float32))
            old = m0[rows, :]
            m = jnp.maximum(old, jnp.max(top, axis=1, keepdims=True) * SCALE)
            factor = jnp.exp2(old - m)
            m1[rows, :] = m
            acc1[rows, :] = acc0[rows, :] * jnp.concatenate([factor, factor], axis=1)
        lax.fori_loop(0, blocks, block, none)

    if last:
        ok = lax.broadcasted_iota(jnp.int32, (CAP, HD), 0) < live
        for h in range(GROUP):
            at = slice(h * CAP, (h + 1) * CAP)
            total = jnp.sum(acc1[at, HD : 2 * HD], axis=1, keepdims=True)
            result = jnp.where(ok, acc1[at, 0:HD] / total, 0.0)
            out_ref[:, h * HD : (h + 1) * HD] = result.astype(jnp.bfloat16)


def attention(first, last, count, live, sources, state, interpret=False):
    talls = [ROWS_B if s.shape[1] == TALL_B else ROWS_A for s in sources]
    counts = [s.shape[0] for s in sources]
    keys = sum(c * t for c, t in zip(counts, talls))
    height = (keys // WIDTH + 2) * WIDTH
    vmem = pl.BlockSpec(memory_space=pltpu.VMEM)
    smem = pl.BlockSpec(memory_space=pltpu.SMEM)
    state_shapes = [
        ((ROWS, HD), jnp.float32),
        ((ROWS, 2 * HD), jnp.float32),
    ]
    scratch_state = [pltpu.VMEM(*s) for s in state_shapes]
    if last:
        out_shape = jax.ShapeDtypeStruct((CAP, GROUP * HD), jnp.bfloat16)
        out_specs = vmem
    else:
        out_shape = [jax.ShapeDtypeStruct(*s) for s in state_shapes]
        out_specs = [vmem] * 2
    scratch = (
        (scratch_state if last else [])
        + [
            pltpu.VMEM((ROWS, HD), jnp.bfloat16),
            pltpu.VMEM((height, HD), jnp.bfloat16),
            pltpu.VMEM((height, 2 * HD), jnp.bfloat16),
            pltpu.SemaphoreType.DMA((len(sources),)),
        ]
        + [pltpu.VMEM(s.shape, jnp.bfloat16) for s in sources]
        + (scratch_state if first else [])
    )

    def kernel(*refs):
        attention_kernel(first, last, talls, counts, *refs)

    return pl.pallas_call(
        kernel,
        out_shape=out_shape,
        in_specs=[smem, smem] + [pl.BlockSpec(memory_space=pl.ANY)] * len(sources)
        + [vmem] * len(state),
        out_specs=out_specs,
        scratch_shapes=scratch,
        compiler_params=pltpu.CompilerParams(vmem_limit_bytes=VMEM_LIMIT),
        cost_estimate=pl.CostEstimate(
            flops=8 * ROWS * keys * HD, bytes_accessed=8 << 20, transcendentals=0
        ),
        interpret=interpret,
    )(count, live, *sources, *state)


def early_attention(own, beside, count_b, live, arrays, interpret=False):
    state = attention(True, False, count_b[:16], live, own, arrays, interpret)
    state = (arrays[0], *state)
    state = attention(False, False, count_b[16:48], live, beside, state, interpret)
    return (arrays[0], *state)


def late_attention(gathered, across, count_a, count_b, live, state, interpret=False):
    count = jnp.concatenate([count_b[48:], count_a])
    return attention(False, True, count, live, across + [gathered], state, interpret)


def select_kernel(n_src, key_ref, value_ref, after_ref, *refs):
    sources, (out_ref, pages, sems) = refs[:n_src], refs[n_src:]
    copies = []
    start = 0
    for i, source in enumerate(sources):
        count = source.shape[0]
        copies.append(
            pltpu.make_async_copy(source, pages.at[pl.ds(start, count)], sems.at[i])
        )
        start += count
    for copy in copies:
        copy.start()
    for copy in copies:
        copy.wait()

    def one(s, carry):
        place = key_ref[s]
        keep = jnp.where(place >= 0, 1.0, 0.0).astype(jnp.bfloat16)
        out_ref[s, :, 0:HD] = pages[jnp.maximum(place, 0)] * keep
        out_ref[s, :, HD : 2 * HD] = pages[jnp.maximum(value_ref[s], 0)] * keep
        return carry

    lax.fori_loop(0, 2 * N, one, 0, unroll=4)


def select_pages(places, sources, after, interpret=False):
    sources = [s.reshape(s.shape[0] * s.shape[1] // PAGE, PAGE, HD) for s in sources]
    total = sum(s.shape[0] for s in sources)
    smem = pl.BlockSpec(memory_space=pltpu.SMEM)
    anywhere = pl.BlockSpec(memory_space=pl.ANY)

    def kernel(*refs):
        select_kernel(len(sources), *refs)

    return pl.pallas_call(
        kernel,
        out_shape=jax.ShapeDtypeStruct((2 * N, PAGE, 2 * HD), jnp.bfloat16),
        in_specs=[smem] * 2 + [anywhere] * (1 + len(sources)),
        out_specs=pl.BlockSpec(memory_space=pltpu.VMEM),
        scratch_shapes=[
            pltpu.VMEM((total, PAGE, HD), jnp.bfloat16),
            pltpu.SemaphoreType.DMA((len(sources),)),
        ],
        compiler_params=pltpu.CompilerParams(vmem_limit_bytes=VMEM_LIMIT),
        cost_estimate=pl.CostEstimate(flops=0, bytes_accessed=8 << 20, transcendentals=0),
        interpret=interpret,
    )(*places, after, *sources)


def payload_kernel(k_ref, v_ref, owner_ref, a_ref, b_ref):
    a_ref[0:ROWS_A, :] = k_ref[0:ROWS_A, :]
    a_ref[ROWS_A : 2 * ROWS_A, :] = v_ref[0:ROWS_A, :]
    a_ref[2 * ROWS_A :, :] = jnp.zeros((PAD, HD), jnp.bfloat16)
    owner = jnp.broadcast_to(owner_ref[...].astype(jnp.float32), (PAD, PAGES))
    a_ref[2 * ROWS_A :, 0:PAGES] = owner.astype(jnp.bfloat16)
    b_ref[0:ROWS_B, :] = k_ref[ROWS_A:, :]
    b_ref[ROWS_B:, :] = v_ref[ROWS_A:, :]


def payloads(keys, values, page_owner, interpret=False):
    vmem = pl.BlockSpec(memory_space=pltpu.VMEM)
    return pl.pallas_call(
        payload_kernel,
        out_shape=[
            jax.ShapeDtypeStruct((TALL_A, HD), jnp.bfloat16),
            jax.ShapeDtypeStruct((TALL_B, HD), jnp.bfloat16),
        ],
        in_specs=[vmem] * 3,
        out_specs=[vmem] * 2,
        interpret=interpret,
    )(keys, values, page_owner.reshape(1, PAGES))


def layout(me):
    mx, mz = me // NZ, me % NZ
    dx = jnp.array([0] * 16 + [-1] * 16 + [1] * 16 + [2] * 16, jnp.int32)
    dz = jnp.array(Z_ALL * NX, jnp.int32)
    piece_b = ((mx + dx + NX) % NX) * NZ + (mz + dz + NZ) % NZ
    dx = jnp.array(X_ORDER * NZ, jnp.int32)
    piece_a = ((mx + dx + NX) % NX) * NZ + jnp.arange(N, dtype=jnp.int32) // NX
    return piece_a, piece_b


def pick(table, index):
    place = jnp.arange(N, dtype=jnp.int32)
    return jnp.sum(jnp.where(index[:, None] == place[None, :], table[None, :], 0), axis=1)


def inverse(index):
    place = jnp.arange(N, dtype=jnp.int32)
    return jnp.sum(jnp.where(index[None, :] == place[:, None], place[None, :], 0), axis=1)


def page_places(me, gathered, piece_a, piece_b, lengths):
    place = jnp.arange(N, dtype=jnp.int32)
    owners = gathered[:, 2 * ROWS_A, :PAGES]
    page = jnp.arange(PAGES, dtype=jnp.int32)[None, :]
    match = owners == me.astype(jnp.bfloat16)
    low = jnp.min(jnp.where(match, page, PAGES), axis=1)
    high = jnp.max(jnp.where(match, page, -1), axis=1)
    pages = jnp.stack([low, jnp.where(high > low, high, PAGES)], axis=1)
    hit = piece_a[None, :] == place[:, None]
    pages = jnp.sum(jnp.where(hit[:, :, None], pages[None, :, :], 0), axis=1)
    at_a = N * (TALL_B // PAGE) + inverse(piece_a)[:, None] * (TALL_A // PAGE) + pages
    at_b = inverse(piece_b)[:, None] * (TALL_B // PAGE) + pages - PAGES_A
    in_a = pages < PAGES_A
    key_place = jnp.where(in_a, at_a, at_b)
    value_place = key_place + jnp.where(in_a, PAGES_A, PAGES_B)
    finished = (pages < PAGES) & ((pages + 1) * PAGE <= lengths[:, None])
    key_place = jnp.where(finished, key_place, -1)
    value_place = jnp.where(finished, value_place, -1)
    return key_place.reshape(2 * N), value_place.reshape(2 * N)


def live_counts(me, lengths, piece_a, piece_b):
    count_a = jnp.where(piece_a < me, jnp.minimum(pick(lengths, piece_a), ROWS_A), 0)
    count_b = jnp.where(piece_b < me, jnp.maximum(pick(lengths, piece_b) - ROWS_A, 0), 0)
    return count_a, count_b


def body(queries, keys, values, lengths, page_owner):
    me = lax.axis_index("ctx")
    live = jnp.sum(jnp.where(jnp.arange(N, dtype=jnp.int32) == me, lengths, 0)).reshape(1)
    gathered, own, beside, across = exchange(*payloads(keys, values, page_owner))
    piece_a, piece_b = layout(me)
    own, lengths = lax.optimization_barrier((own, lengths))
    count_a, count_b = live_counts(me, lengths, piece_a, piece_b)
    key_place, value_place = page_places(me, gathered, piece_a, piece_b, lengths)
    state = early_attention(own, beside, count_b, live, (queries, keys, values))
    outgoing = select_pages(
        (key_place, value_place), own + beside + across + [gathered], state[1]
    )
    decode_cache = lax.all_to_all(
        outgoing.reshape(2 * N, PAGE, 1, 2 * HD), "tp", split_axis=0, concat_axis=2, tiled=True
    )
    attended = late_attention(gathered, across, count_a, count_b, live, state)
    return (attended, decode_cache.reshape((1,) + decode_cache.shape))


def solution(mesh):
    in_specs = (P("ctx", "tp"), P("ctx", "tp"), P("ctx", "tp"), P(), P("ctx", None))
    out_specs = (P("ctx", "tp"), P("ctx", "tp", None, None, None))
    return jax.shard_map(body, mesh=mesh, in_specs=in_specs, out_specs=out_specs, check_vma=False)
```
